256 devices in a mesh: seq: 16 (over z, core), exp: 16 (over y, x).
Axes of the slice: x: 4, y: 4, z: 8, core: 2. Of those that a mesh axis runs over, the one named last changes fastest.
Arguments:
- queries: bfloat16 [16, 2048, 4096], P('exp', 'seq'), may hold values from -65 to 65
- keys: bfloat16 [16, 2048, 256], P('exp', 'seq'), may hold values from -5 to 5
- values: bfloat16 [16, 2048, 256], P('exp', 'seq'), may hold values from -6 to 6
- attn_out: bfloat16 [16, 2048, 4096], P('exp', 'seq'), may hold values from -6 to 6
- d_attn: bfloat16 [16, 2048, 4096], P('exp', 'seq'), may hold values from -6 to 6
- normed: bfloat16 [16, 2048, 2048], P('exp', 'seq'), may hold values from -6 to 6
- d_moe: bfloat16 [16, 2048, 2048], P('exp', 'seq'), may hold values from -6 to 6
- expert_ids: int32 [16, 2048, 8], P('exp', 'seq'), may hold values from 0 to 127, all different within a row; in each aligned block of 128 rows (0 to 127, 128 to 255, ..., all dimensions but the last counted through in order) at most 10 rows name the same one
- route_weight: float32 [16, 2048, 8], P('exp', 'seq'), may hold values from 0.05 to 0.5
- gate_w: bfloat16 [16, 2048, 1536], P('exp', 'seq'), may hold values from -0.125 to 0.125
- up_w: bfloat16 [16, 2048, 1536], P('exp', 'seq'), may hold values from -0.125 to 0.125
- down_t: bfloat16 [16, 2048, 1536], P('exp', 'seq'), may hold values from -0.15625 to 0.15625
Outputs:
- d_queries: bfloat16 [16, 2048, 4096], P('exp', 'seq')
- key_gradient: bfloat16 [16, 2048, 256], P('exp', 'seq')
- value_gradient: bfloat16 [16, 2048, 256], P('exp', 'seq')
- d_normed: bfloat16 [16, 2048, 2048], P('exp', 'seq')
The draws below stay inside these ranges and needn't reach their ends.
Inputs may be any that keep to these rules, and one draw needn't show every extreme that they name: `expert_ids`: in the 128 rows of one device no expert is named more than 10 times, a bound that some block reaches.
All inputs are finite; a program needn't handle non-finite values.
Results may differ from the reference program's by a relative error of at most 0.0057.
Values may be sent and summed in bfloat16 or wider, within the bound.
A program may use at most 192 MiB of HBM per device.

```python
import math
import jax
import jax.numpy as jnp
import numpy as np
from jax import lax

D = 2048
QUERY_HEADS = 32
KEY_VALUE_HEADS = 2
HEAD_SIZE = 128
HID = 1536
EXPERTS = 128
TOPK = 8
TOK_DEV = 128
SEQUENCE_TOKENS = 2048
SEQUENCE_COUNT = 16
EXP_FLIGHT = 16
CAP = 10
N_SEQ = 16
N_EXP = 16


def shared_keys(key):
    return jax.random.truncated_normal(key, -5.0, 5.0, (SEQUENCE_COUNT, SEQUENCE_TOKENS, KEY_VALUE_HEADS * HEAD_SIZE), jnp.float32)


def draw_keys(key, part):
    common_heads = shared_keys(key)
    return common_heads.astype(jnp.bfloat16)


def draw_queries(key, part):
    key = jax.random.fold_in(key, 22)
    fresh = jax.random.truncated_normal(key, -5.0, 5.0, (SEQUENCE_COUNT, SEQUENCE_TOKENS, QUERY_HEADS * HEAD_SIZE), jnp.float32)
    return fresh.astype(jnp.bfloat16)


def steps_of(own_key, dims, cuts, smallest, largest):
    def one(position, blocks):
        heights = jax.random.uniform(jax.random.fold_in(jax.random.fold_in(own_key, 6), position), (blocks,), jnp.float32, smallest / len(cuts), largest / len(cuts))
        return jnp.repeat(jnp.exp(heights), dims[position] // blocks).reshape((-1,) + (1,) * (len(dims) - position - 1))

    level = one(*cuts[0])
    for cut in cuts[1:]:
        level = level * one(*cut)
    return level


def shared_out(stream_key, own, number, rows, amount, top, reach, slope):
    ranking = jax.random.permutation(stream_key, amount)
    heavy_load, usual = portions_of(amount, rows * top, reach, slope, True), portions_of(amount, rows * top, reach, slope, False)
    places = jnp.arange(amount)

    def named(tallies, rotation):
        used = int((tallies > 0).sum())
        fixed = max(1, used // 4)
        shifted = fixed + (places - fixed + rotation * (used - fixed)) % max(1, amount - fixed)
        return jnp.zeros((amount,), jnp.int32).at[ranking[jnp.where(places < fixed, places, shifted)]].set(jnp.asarray(tallies, jnp.int32))

    tallies = jnp.where(number % 4 == 0, named(heavy_load, number // 4), named(usual, number - number // 4 - 1))
    mixed = jax.random.permutation(jax.random.fold_in(own, 3), amount)
    donor, sink = mixed[0:amount // 2 * 2:2], mixed[1:amount // 2 * 2:2]
    margin = jnp.minimum(tallies[donor] - 1, reach - tallies[sink]) // 2
    margin = jnp.where((donor == ranking[0]) | (sink == ranking[0]) | (tallies[sink] == 0), 0, jnp.maximum(margin, 0))
    shifted = jax.random.randint(jax.random.fold_in(own, 4), (amount // 2,), 0, 1 << 20) % (margin + 1)
    tallies = tallies.at[donor].add(-shifted).at[sink].add(shifted)
    items = jnp.searchsorted(jnp.cumsum(tallies), jnp.arange(rows * top), side="right").astype(jnp.int32)
    table = items.reshape(top, rows).T
    table = table[jax.random.permutation(jax.random.fold_in(own, 1), rows)]
    rotation = jax.random.randint(jax.random.fold_in(own, 2), (rows, 1), 0, top)
    return jnp.take_along_axis(table, (jnp.arange(top)[None, :] + rotation) % top, axis=1)


def portions_of(count, total, most, slope, full):
    loads = [(1 << 20) // math.isqrt(rank ** slope) + 1 for rank in range(1, count + 1)]
    largest = most if full else min(most, max(-(-total // count), total * loads[0] // sum(loads)))
    least = 1 if total - largest >= count - 1 else 0
    given, rest = [largest] + [least] * (count - 1), total - largest - least * (count - 1)
    while rest > 0:
        free = [i for i in range(1, count) if given[i] < largest] or [i for i in range(1, count) if given[i] < most]
        mass, left = sum([loads[i] for i in free]), rest
        for i in free:
            more = min(most - given[i], max(1, left * loads[i] // mass), rest)
            given[i] = given[i] + more
            rest = rest - more
    return np.array(given)


def scatter_about(own_key, dims, scale, reach, split=(), kind=jnp.bfloat16):
    gain = steps_of(own_key, dims, split, -0.22, 0.18) if split else 1.0
    array = jax.random.normal(own_key, dims, jnp.float32) * scale * gain
    return jnp.minimum(jnp.maximum(array, -reach), reach).astype(kind)


def setup_inputs(seed: int = 0) -> dict:
    key_list = jax.random.split(jax.random.key(seed), 13)
    queries = draw_queries(jax.random.fold_in(key_list[12], 71), 0)
    keys = draw_keys(jax.random.fold_in(key_list[12], 71), 0)
    values = scatter_about(key_list[2], (SEQUENCE_COUNT, SEQUENCE_TOKENS, KEY_VALUE_HEADS * HEAD_SIZE), 1.0, 6.0, ((0, 16), (1, 16)))
    attn_out = scatter_about(key_list[3], (SEQUENCE_COUNT, SEQUENCE_TOKENS, QUERY_HEADS * HEAD_SIZE), 1.0, 6.0, ((0, 16), (1, 16)))
    d_attn = scatter_about(key_list[4], (SEQUENCE_COUNT, SEQUENCE_TOKENS, QUERY_HEADS * HEAD_SIZE), 1.0, 6.0, ((0, 16), (1, 16)))
    normed = scatter_about(key_list[5], (SEQUENCE_COUNT, SEQUENCE_TOKENS, D), 1.0, 6.0, ((0, 16), (1, 16)))
    d_moe = scatter_about(key_list[6], (SEQUENCE_COUNT, SEQUENCE_TOKENS, D), 1.0, 6.0, ((0, 16), (1, 16)))
    expert_ids_keys = jax.random.split(jax.random.fold_in(key_list[7], 1), SEQUENCE_COUNT * SEQUENCE_TOKENS // TOK_DEV)
    expert_ids_turns = jax.random.permutation(jax.random.fold_in(key_list[7], 3), SEQUENCE_COUNT * SEQUENCE_TOKENS // TOK_DEV)
    expert_ids = jax.vmap(lambda own, number: shared_out(jax.random.fold_in(key_list[7], 2), own, number, TOK_DEV, EXPERTS, TOPK, CAP, 2))(expert_ids_keys, expert_ids_turns).reshape((SEQUENCE_COUNT, SEQUENCE_TOKENS, TOPK))
    route_weight = jnp.clip(jnp.exp(math.log(0.5) - 2.3025851 * jax.random.uniform(key_list[8], (SEQUENCE_COUNT, SEQUENCE_TOKENS, TOPK), jnp.float32) ** steps_of(key_list[8], (SEQUENCE_COUNT, SEQUENCE_TOKENS, TOPK), ((0, 16), (1, 16)), -0.2, 0.2)), 0.05, 0.5)
    gate_w = scatter_about(key_list[9], (EXP_FLIGHT, D, HID), D ** -0.5, 0.125, ((0, 16), (1, 16)))
    up_w = scatter_about(key_list[10], (EXP_FLIGHT, D, HID), D ** -0.5, 0.125, ((0, 16), (1, 16)))
    down_t = scatter_about(key_list[11], (EXP_FLIGHT, D, HID), HID ** -0.5, 0.15625, ((0, 16), (1, 16)))
    return {"queries": queries, "keys": keys, "values": values, "attn_out": attn_out, "d_attn": d_attn, "normed": normed, "d_moe": d_moe, "expert_ids": expert_ids, "route_weight": route_weight, "gate_w": gate_w, "up_w": up_w, "down_t": down_t}


highest = lax.Precision.HIGHEST

def head_gradients(query_heads, key_heads, value_heads, output_heads, grad_heads):
    length, head_count, head_width = query_heads.shape
    scaling = 1.0 / math.sqrt(head_width)
    block_size = min(512, length)
    query_parts = []
    key_grad = jnp.zeros((length, head_count, head_width), jnp.float32)
    value_grad = jnp.zeros((length, head_count, head_width), jnp.float32)
    for start_row in range(0, length, block_size):
        stop_row = start_row + block_size
        query_block = query_heads[start_row:stop_row].astype(jnp.float32)
        key_block = key_heads[:stop_row].astype(jnp.float32)
        value_block = value_heads[:stop_row].astype(jnp.float32)
        grad_block = grad_heads[start_row:stop_row].astype(jnp.float32)
        output_block = output_heads[start_row:stop_row].astype(jnp.float32)
        scores = jnp.einsum('qhd,khd->hqk', query_block, key_block, precision=highest) * scaling
        row_pos = start_row + jnp.arange(block_size, dtype=jnp.int32)[:, None]
        col_pos = jnp.arange(stop_row, dtype=jnp.int32)[None, :]
        scores = jnp.where(col_pos <= row_pos, scores, -jnp.inf)
        row_max = lax.optimization_barrier(jnp.max(scores, axis=-1, keepdims=True))
        log_total = row_max + jnp.log(lax.optimization_barrier(jnp.sum(jnp.exp(scores - row_max), axis=-1, keepdims=True)))
        weights = jnp.exp(scores - log_total)
        weights_low = lax.optimization_barrier(weights.astype(jnp.bfloat16)).astype(jnp.float32)
        row_dot = lax.optimization_barrier(jnp.sum(grad_block * output_block, axis=-1))
        grad_weights = jnp.einsum('qhd,khd->hqk', grad_block, value_block, precision=highest)
        grad_scores = (weights * (grad_weights - row_dot.T[:, :, None])).astype(jnp.bfloat16)
        grad_scores = lax.optimization_barrier(grad_scores).astype(jnp.float32)
        query_parts.append((jnp.einsum('hqk,khd->qhd', grad_scores, key_block, precision=highest) * scaling).astype(jnp.bfloat16))
        key_grad = key_grad.at[:stop_row].add(jnp.einsum('hqk,qhd->khd', grad_scores, query_block, precision=highest) * scaling)
        value_grad = value_grad.at[:stop_row].add(jnp.einsum('hqk,qhd->khd', weights_low, grad_block, precision=highest))
    return (jnp.concatenate(query_parts, axis=0), key_grad, value_grad)

def expert_rows(token_rows, grad_rows, gate_piece, up_piece, down_piece):
    gate_val = jnp.dot(token_rows, gate_piece, preferred_element_type=jnp.float32)
    up_val = jnp.dot(token_rows, up_piece, preferred_element_type=jnp.float32)
    hidden_grad = jnp.dot(grad_rows, down_piece, preferred_element_type=jnp.float32)
    sigmoid = jax.nn.sigmoid(gate_val)
    activated = gate_val * sigmoid
    gate_grad = (hidden_grad * up_val * sigmoid * (1.0 + gate_val * (1.0 - sigmoid))).astype(jnp.bfloat16)
    up_grad = (hidden_grad * activated).astype(jnp.bfloat16)
    return jnp.dot(gate_grad, gate_piece.T, preferred_element_type=jnp.float32) + jnp.dot(up_grad, up_piece.T, preferred_element_type=jnp.float32)

def reference(queries, keys, values, attn_out, d_attn, normed, d_moe, expert_ids, route_weight, gate_w, up_w, down_t):
    query_group_width = QUERY_HEADS // KEY_VALUE_HEADS
    query_list, key_collection, value_collection = ([], [], [])
    for sequence_index in range(SEQUENCE_COUNT):
        query_seq = queries[sequence_index].reshape(SEQUENCE_TOKENS, QUERY_HEADS, HEAD_SIZE)
        sequence_keys = jnp.repeat(keys[sequence_index].reshape(SEQUENCE_TOKENS, KEY_VALUE_HEADS, HEAD_SIZE), query_group_width, axis=1)
        sequence_values = jnp.repeat(values[sequence_index].reshape(SEQUENCE_TOKENS, KEY_VALUE_HEADS, HEAD_SIZE), query_group_width, axis=1)
        output_seq = attn_out[sequence_index].reshape(SEQUENCE_TOKENS, QUERY_HEADS, HEAD_SIZE)
        grad_seq = d_attn[sequence_index].reshape(SEQUENCE_TOKENS, QUERY_HEADS, HEAD_SIZE)
        grad_q, key_gradient_part, value_gradient_part = head_gradients(query_seq, sequence_keys, sequence_values, output_seq, grad_seq)
        query_list.append(grad_q.reshape(SEQUENCE_TOKENS, QUERY_HEADS * HEAD_SIZE))
        key_collection.append(key_gradient_part.reshape(SEQUENCE_TOKENS, KEY_VALUE_HEADS, query_group_width, HEAD_SIZE).sum(2).reshape(SEQUENCE_TOKENS, KEY_VALUE_HEADS * HEAD_SIZE).astype(jnp.bfloat16))
        value_collection.append(value_gradient_part.reshape(SEQUENCE_TOKENS, KEY_VALUE_HEADS, query_group_width, HEAD_SIZE).sum(2).reshape(SEQUENCE_TOKENS, KEY_VALUE_HEADS * HEAD_SIZE).astype(jnp.bfloat16))
    d_queries = jnp.stack(query_list)
    key_gradient = jnp.stack(key_collection)
    value_gradient = jnp.stack(value_collection)
    blocks = SEQUENCE_COUNT * N_SEQ
    token_blocks = normed.reshape(blocks, TOK_DEV, D).astype(jnp.float32)
    grad_blocks = d_moe.reshape(blocks, TOK_DEV, D).astype(jnp.float32)
    id_blocks = expert_ids.reshape(blocks, TOK_DEV * TOPK)
    weight_blocks = route_weight.reshape(blocks, TOK_DEV * TOPK)
    slot_index = jnp.arange(CAP, dtype=jnp.int32)
    result = jnp.zeros((blocks, TOK_DEV, D), jnp.float32)
    for expert in range(N_EXP):
        named_mask = (id_blocks == expert).astype(jnp.int32)
        slot_rank = jnp.cumsum(named_mask, axis=1, dtype=jnp.int32) - 1
        chosen = ((named_mask[:, None, :] == 1) & (slot_rank[:, None, :] == slot_index[None, :, None])).astype(jnp.float32)
        select = chosen.reshape(blocks, CAP, TOK_DEV, TOPK).sum(-1)
        mixing = (chosen * weight_blocks[:, None, :]).reshape(blocks, CAP, TOK_DEV, TOPK).sum(-1)
        token_rows = jnp.einsum('bct,btd->bcd', select, token_blocks, precision=highest).astype(jnp.bfloat16).reshape(blocks * CAP, D)
        grad_rows = jnp.einsum('bct,btd->bcd', select, grad_blocks, precision=highest).astype(jnp.bfloat16).reshape(blocks * CAP, D)
        assign_grad = expert_rows(token_rows, grad_rows, gate_w[expert], up_w[expert], down_t[expert]).astype(jnp.bfloat16)
        assign_grad = lax.optimization_barrier(assign_grad).astype(jnp.float32).reshape(blocks, CAP, D)
        result = result + jnp.einsum('bct,bcd->btd', mixing, assign_grad, precision=highest)
    d_normed = result.reshape(SEQUENCE_COUNT, SEQUENCE_TOKENS, D).astype(jnp.bfloat16)
    return (d_queries, key_gradient, value_gradient, d_normed)
```

```python
import functools
import math

import jax
import jax.numpy as jnp
from jax import lax
from jax.experimental import pallas as pl
from jax.experimental.pallas import tpu as pltpu
from jax.sharding import PartitionSpec as P

MESH = pl.DeviceIdType.MESH
F32 = jnp.float32
BF16 = jnp.bfloat16
HEAD = 128
TOK = 128
PAIR = 2 * TOK
SLOT = 16
LOW = -1e30
MINOR = (((1,), (1,)), ((), ()))
MAJOR = (((0,), (0,)), ((), ()))


def dot(a, b, dims=(((1,), (0,)), ((), ()))):
    return lax.dot_general(a, b, dims, preferred_element_type=F32)


def kernel(
    nz, ne,
    q_in, k_in, v_in, o_in, do_in, x_in, g_in, ids, route, gate_in, up_in, down_in,
    dq_out, dk_out, dv_out, dn_out,
    W, KV, KT, Q, DO, OF, DOF, RDX, RD, PB, MJ, DKV, DQT, DQ, SB, RB, FB, XG, XS, XR, ACC, GU, RS, RR, MIX, OUT,
    loc, sib_s, sib_r, wgt_s, wgt_r, wsb_s, wsb_r, kv_s, kv_r, gr_s, gr_r, tok_s, tok_r, ret_s, ret_r,
):
    half = nz // 2
    nk = 3 * half
    groups = Q.shape[1] // HEAD
    width = groups * HEAD
    hid = W.shape[3]
    model = W.shape[1] * W.shape[2]
    scale = 1.0 / math.sqrt(HEAD)
    log2e = math.log2(math.e)

    s = lax.axis_index("seq")
    e = lax.axis_index("exp")
    z = lax.div(s, 2)
    c = lax.rem(s, 2)
    other = 1 - c

    def plane(delta):
        return lax.rem(z + delta + nz, nz)

    near = (
        {"seq": 2 * plane(1) + c},
        {"seq": 2 * plane(-1) + c},
    )
    sibling = {"seq": 2 * z + other}

    def peer(p):
        return lax.rem(e + p, ne)

    def send(src, dst, ss, rs, to):
        return pltpu.make_async_remote_copy(
            src_ref=src, dst_ref=dst, send_sem=ss, recv_sem=rs, device_id=to, device_id_type=MESH
        )

    def arrived(dst, rs):
        send(dst, dst, rs, rs, sibling).wait_recv()

    def sent(src, ss):
        send(src, src, ss, ss, sibling).wait_send()

    mine = pl.ds(pl.multiple_of(c * TOK, TOK), TOK)
    theirs = pl.ds(pl.multiple_of(other * TOK, TOK), TOK)
    my_heads = pl.ds(pl.multiple_of(c * width, width), width)
    their_heads = pl.ds(pl.multiple_of(other * width, width), width)
    my_head = pl.ds(pl.multiple_of(c * HEAD, HEAD), HEAD)
    their_head = pl.ds(pl.multiple_of(other * HEAD, HEAD), HEAD)

    local = [
        (k_in.at[0, :, my_head], KV.at[z, 0, mine]),
        (v_in.at[0, :, my_head], KV.at[z, 1, mine]),
        (x_in.at[0], XG.at[0]),
        (g_in.at[0], XG.at[1]),
        (o_in.at[0], OF),
        (do_in.at[0], DOF),
        (q_in.at[0, :, my_heads], Q.at[mine]),
        (do_in.at[0, :, my_heads], DO.at[mine]),
        (gate_in.at[0], W.at[0, s]),
        (up_in.at[0], W.at[1, s]),
        (down_in.at[0], W.at[2, s]),
    ]
    local = [pltpu.make_async_copy(a, b, loc.at[i]) for i, (a, b) in enumerate(local)]
    for copy in local:
        copy.start()

    barrier = pltpu.get_barrier_semaphore()
    for to in (*near, sibling):
        pl.semaphore_signal(barrier, inc=1, device_id=to, device_id_type=MESH)

    def greet(p, carry):
        pl.semaphore_signal(barrier, inc=1, device_id={"exp": peer(p)}, device_id_type=MESH)
        return carry

    lax.fori_loop(1, ne, greet, 0)
    pl.semaphore_wait(barrier, 3 + ne - 1)

    swap = [
        send(k_in.at[0, :, their_head], KV.at[z, 0, mine], sib_s.at[0], sib_r.at[0], sibling),
        send(v_in.at[0, :, their_head], KV.at[z, 1, mine], sib_s.at[1], sib_r.at[1], sibling),
        send(q_in.at[0, :, their_heads], Q.at[mine], sib_s.at[2], sib_r.at[2], sibling),
        send(do_in.at[0, :, their_heads], DO.at[mine], sib_s.at[3], sib_r.at[3], sibling),
    ]
    for copy in swap:
        copy.start()

    def kv_region(d, hop):
        at = plane(-hop if d == 0 else hop)
        return KV.at[at] if hop < half else KV.at[at, d]

    def kv_forward(d, hop):
        at = plane(-hop if d == 0 else hop)
        region = KV.at[at] if hop + 1 < half else KV.at[at, d]
        send(region, region, kv_s.at[d, hop], kv_r.at[d, hop], near[d]).start()

    def kv_sent(d, hop):
        at = plane(-hop if d == 0 else hop)
        region = KV.at[at] if hop + 1 < half else KV.at[at, d]
        sent(region, kv_s.at[d, hop])

    def kv_step(hop):
        for d in range(2):
            arrived(kv_region(d, hop), kv_r.at[d, hop - 1])
            if hop < half:
                kv_forward(d, hop)

    own = (gate_in, up_in, down_in)

    def w_own(d, m):
        return send(own[m].at[0], W.at[m, s], wgt_s.at[d, m], wgt_r.at[d, m], near[d])

    def w_own_sibling(m):
        return send(own[m].at[0], W.at[m, s], wsb_s.at[0, nk + m], wsb_r.at[0, nk + m], sibling)

    def w_region(d, k, core, rows_of=None):
        hop = lax.div(k, 3) + 1
        at = plane(-hop if d == 0 else hop)
        region = W.at[lax.rem(k, 3), 2 * at + core]
        if rows_of is None:
            return region
        rows = W.shape[2] // 2
        return region.at[pl.ds(rows * rows_of, rows)]

    def w_arrives(d, k, core):
        last = not isinstance(k, jax.Array) and k >= nk - 3
        return w_region(d, k, core, d if last else None)

    def w_leaves(d, k):
        last = not isinstance(k, jax.Array) and k + 3 >= nk - 3
        return w_region(d, k, c, d if last else None)

    def pump(k):
        for d in range(2):
            region = w_arrives(d, k, c)
            arrived(region, wgt_r.at[d, k])
            if isinstance(k, jax.Array) or k + 3 < nk:
                leaving = w_leaves(d, k)
                send(leaving, leaving, wgt_s.at[d, k + 3], wgt_r.at[d, k + 3], near[d]).start()
            send(region, region, wsb_s.at[d, k], wsb_r.at[d, k], sibling).start()

    def routing():
        lane = lax.broadcasted_iota(jnp.int32, (TOK, ne * SLOT), 1)
        expert = lax.shift_right_logical(lane, 4)
        slot = lax.bitwise_and(lane, SLOT - 1).astype(F32)
        named = jnp.zeros((TOK, ne * SLOT), F32)
        weight = jnp.zeros((TOK, ne * SLOT), F32)
        for rank in range(ids.shape[2]):
            hit = ids[0, :, rank : rank + 1] == expert
            named = jnp.where(hit, 1.0, named)
            weight = jnp.where(hit, route[0, :, rank : rank + 1], weight)
        row = lax.broadcasted_iota(jnp.int32, (TOK, TOK), 0)
        col = lax.broadcasted_iota(jnp.int32, (TOK, TOK), 1)
        earlier = (col < row).astype(F32).astype(BF16)
        place = dot(earlier, named.astype(BF16))
        select = jnp.where((named > 0.0) & (place == slot), 1.0, 0.0)
        mixing = select * weight
        high = mixing.astype(BF16)
        MIX[0] = high
        MIX[1] = (mixing - high.astype(F32)).astype(BF16)
        return select.astype(BF16)

    def token_copy(p):
        to = peer(p)
        return send(
            XS.at[:, pl.ds(pl.multiple_of(to * SLOT, SLOT), SLOT)],
            XR.at[:, pl.ds(pl.multiple_of(e * SLOT, SLOT), SLOT)],
            tok_s.at[p], tok_r.at[p], {"exp": to},
        )

    def token_arrived(p):
        src = lax.rem(e - p + ne, ne)
        arrived(XR.at[:, pl.ds(pl.multiple_of(src * SLOT, SLOT), SLOT)], tok_r.at[p])

    def loop(lo, hi, f):
        def body(i, carry):
            f(i)
            return carry

        lax.fori_loop(lo, hi, body, 0)

    local[0].wait()
    local[1].wait()
    arrived(KV.at[z, 0, theirs], sib_r.at[0])
    arrived(KV.at[z, 1, theirs], sib_r.at[1])
    for d in range(2):
        kv_forward(d, 0)
    for m in range(3):
        w_own_sibling(m).start()
    local[2].wait()
    local[3].wait()
    select = routing()
    for i in range(2):
        for n in range(model // 512):
            cols = pl.ds(512 * n, 512)
            XS[i, :, cols] = dot(select, XG[i, :, cols], MAJOR).astype(BF16)
    loop(1, ne, lambda p: token_copy(p).start())
    my_slots = pl.ds(pl.multiple_of(e * SLOT, SLOT), SLOT)
    XR[:, my_slots, :] = XS[:, my_slots, :]
    kv_step(1)
    for d in range(2):
        w_own(d, 0).start()

    local[4].wait()
    local[5].wait()
    ones = jnp.ones((8, HEAD), BF16)

    def head_dot(col):
        cols = pl.ds(pl.multiple_of(col, HEAD), HEAD)
        product = OF[:, cols].astype(F32) * DOF[:, cols].astype(F32)
        high = product.astype(BF16)
        low = (product - high.astype(F32)).astype(BF16)
        return dot(ones, high, MINOR) + dot(ones, low, MINOR)

    def both_dots(h):
        RDX[h] = head_dot((other * groups + h) * HEAD)
        RD[h, :, mine] = head_dot((c * groups + h) * HEAD)

    loop(0, groups, both_dots)
    swap_dot = send(RDX, RD.at[:, :, mine], sib_s.at[4], sib_r.at[4], sibling)
    swap_dot.start()
    kv_step(2)
    for d in range(2):
        w_own(d, 1).start()
    DKV[...] = jnp.zeros(DKV.shape, F32)
    for hop in range(3, half):
        kv_step(hop)
    for d in range(2):
        w_own(d, 2).start()
    if half > 2:
        kv_step(half)

    def turn(j):
        KT[j] = KV[j, 0].T

    loop(0, nz, turn)
    local[6].wait()
    local[7].wait()
    arrived(Q.at[theirs], sib_r.at[2])
    arrived(DO.at[theirs], sib_r.at[3])
    arrived(RD.at[:, :, theirs], sib_r.at[4])

    in_loop = max(0, nk - 6)

    def head(h):
        cols = pl.ds(pl.multiple_of(h * HEAD, HEAD), HEAD)
        queries = Q[:, cols]
        grads = DO[:, cols]
        dots = RD[h]

        def scores(j, carry, diagonal):
            top, total = carry
            value = dot(KV[j, 0], queries, MINOR) * (scale * log2e)
            if diagonal:
                key = lax.broadcasted_iota(jnp.int32, (PAIR, PAIR), 0)
                query = lax.broadcasted_iota(jnp.int32, (PAIR, PAIR), 1)
                value = jnp.where(key <= query, value, LOW)
            value = value.reshape(PAIR // 8, 8, PAIR)
            new = jnp.maximum(top, jnp.max(value, axis=0))
            value = jnp.exp2(value - new[None])
            total = total * jnp.exp2(top - new) + jnp.sum(value, axis=0)
            PB[j] = value.reshape(PAIR, PAIR)
            MJ[j] = new
            return new, total

        carry = (jnp.full((8, PAIR), LOW, F32), jnp.zeros((8, PAIR), F32))
        carry = lax.fori_loop(0, z, lambda j, x: scores(j, x, False), carry)
        top, total = scores(z, carry, True)
        peak = jnp.max(top, axis=0, keepdims=True)
        total = jnp.sum(total * jnp.exp2(top - peak), axis=0, keepdims=True)
        inverse = 1.0 / total
        DQT[...] = jnp.zeros(DQT.shape, F32)

        def gradients(j):
            factor = jnp.exp2(MJ[j] - peak) * inverse
            weights = PB[j].reshape(PAIR // 8, 8, PAIR) * factor[None]
            grad = dot(KV[j, 1], grads, MINOR).reshape(PAIR // 8, 8, PAIR)
            low = (weights * (grad - dots[None])).reshape(PAIR, PAIR).astype(BF16)
            DKV[j, 1] += dot(weights.reshape(PAIR, PAIR).astype(BF16), grads)
            DKV[j, 0] += dot(low, queries)
            DQT[...] += dot(KT[j], low)

        loop(0, z + 1, gradients)
        DQ[:, cols] = (DQT[...] * scale).T.astype(BF16)

        @pl.when((lax.rem(h, 2) == 1) & (lax.div(h, 2) < in_loop))
        def _():
            pump(lax.div(h, 2))

    loop(0, groups, head)

    dq_mine = pltpu.make_async_copy(DQ.at[mine], dq_out.at[0, :, my_heads], loc.at[11])
    dq_theirs = send(DQ.at[theirs], dq_out.at[0, :, my_heads], sib_s.at[5], sib_r.at[5], sibling)
    dq_mine.start()
    dq_theirs.start()

    def grad_step(r):
        for d in range(2):
            t = half - r
            at = plane(r if d == 0 else -r)
            if r == half:
                SB[d, t, d] = DKV[at, d].astype(BF16)
            elif r == half - 1:
                arrived(RB.at[d, t - 1, d], gr_r.at[d, t - 1])
                SB[d, t, d] = (DKV[at, d] + RB[d, t - 1, d].astype(F32)).astype(BF16)
                SB[d, t, 1 - d] = DKV[at, 1 - d].astype(BF16)
            else:
                arrived(RB.at[d, t - 1], gr_r.at[d, t - 1])
                SB[d, t] = (DKV[at] + RB[d, t - 1].astype(F32)).astype(BF16)
            grad_copy(d, t).start()

    def grad_copy(d, t):
        if t == 0:
            return send(SB.at[d, 0, d], RB.at[d, 0, d], gr_s.at[d, 0], gr_r.at[d, 0], near[d])
        return send(SB.at[d, t], RB.at[d, t], gr_s.at[d, t], gr_r.at[d, t], near[d])

    def grad_end():
        t = half - 1
        for d in range(2):
            arrived(RB.at[d, t], gr_r.at[d, t])
        total = DKV[z] + RB[0, t].astype(F32) + RB[1, t].astype(F32)
        FB[0] = (total[0] * scale).astype(BF16)
        FB[1] = total[1].astype(BF16)
        copies = []
        for i, out in enumerate((dk_out, dv_out)):
            copies.append(pltpu.make_async_copy(FB.at[i, mine], out.at[0, :, my_head], loc.at[12 + i]))
            copies.append(send(FB.at[i, theirs], out.at[0, :, my_head], sib_s.at[6 + i], sib_r.at[6 + i], sibling))
        for copy in copies:
            copy.start()
        return copies

    def gather_wait(d, k):
        arrived(w_arrives(d, k, other), wsb_r.at[d, k])

    def add(m, planes, first=False):
        for n in range(hid // 256):
            cols = pl.ds(256 * n, 256)
            total = None if first else ACC[m, :, cols]
            for at in planes:
                part = dot(
                    XR[m // 2, :, pl.ds(pl.multiple_of(at * PAIR, PAIR), PAIR)],
                    W[m, pl.ds(2 * at, 2), :, cols].reshape(PAIR, 256),
                )
                total = part if total is None else total + part
            ACC[m, :, cols] = total

    def add_hop(hop, m):
        k = 3 * (hop - 1) + m
        for d in range(2):
            gather_wait(d, k)
        add(m, [plane(-hop), plane(hop)] if hop < half else [plane(hop)])

    for k in range(in_loop, nk - 6):
        pump(k)
    grad_step(half)
    loop(1, ne, token_arrived)
    for m in range(3):
        local[8 + m].wait()
        arrived(W.at[m, 2 * z + other], wsb_r.at[0, nk + m])
        add(m, [z], first=True)
    rest = list(range(half - 1, 0, -1))
    done = 0
    hops = [(hop, m) for hop in range(1, half + 1) for m in range(3)]
    final = []
    for step in range(nk - 6, nk):
        if rest:
            grad_step(rest.pop(0))
            if not rest:
                final = None
        elif final is None:
            final = grad_end()
        while done < step:
            add_hop(*hops[done])
            done += 1
            if done % 3 == 0:
                break
        pump(step)
    if final is None:
        final = grad_end()
    while done < nk:
        add_hop(*hops[done])
        done += 1

    rows = 16

    def activate(i):
        at = pl.ds(pl.multiple_of(i * rows, rows), rows)
        gate, up, grad = ACC[0, at, :], ACC[1, at, :], ACC[2, at, :]
        sig = 1.0 / (1.0 + jnp.exp(-gate))
        GU[0, at, :] = (grad * up * sig * (1.0 + gate * (1.0 - sig))).astype(BF16)
        GU[1, at, :] = (grad * (gate * sig)).astype(BF16)

    loop(0, ne * SLOT // rows, activate)

    parts = ret_s.shape[0]
    span = model // parts

    def ret_copy(i, p):
        to = peer(p)
        cols = pl.ds(span * i, span)
        return send(
            RS.at[pl.ds(pl.multiple_of(to * SLOT, SLOT), SLOT), cols],
            RR.at[pl.ds(pl.multiple_of(e * SLOT, SLOT), SLOT), cols],
            ret_s.at[i, p], ret_r.at[i, p], {"exp": to},
        )

    def ret_arrived(i, p):
        src = lax.rem(e - p + ne, ne)
        arrived(RR.at[pl.ds(pl.multiple_of(src * SLOT, SLOT), SLOT), pl.ds(span * i, span)], ret_r.at[i, p])

    for i in range(parts):
        for n in range(i * span // PAIR, (i + 1) * span // PAIR):
            back = dot(GU[0], W[0, 2 * n : 2 * n + 2].reshape(PAIR, hid), MINOR) + dot(
                GU[1], W[1, 2 * n : 2 * n + 2].reshape(PAIR, hid), MINOR
            )
            RS[:, PAIR * n : PAIR * n + PAIR] = back.astype(BF16)
        loop(1, ne, lambda p: ret_copy(i, p).start())
        cols = pl.ds(span * i, span)
        RR[my_slots, cols] = RS[my_slots, cols]
    outs = []
    for i in range(parts):
        loop(1, ne, lambda p: ret_arrived(i, p))
        cols = pl.ds(span * i, span)
        back = RR[:, cols]
        OUT[:, cols] = (dot(MIX[0], back) + dot(MIX[1], back)).astype(BF16)
        copy = pltpu.make_async_copy(OUT.at[:, cols], dn_out.at[0, :, cols], loc.at[14 + i])
        copy.start()
        outs.append(copy)

    for copy in swap:
        copy.wait_send()
    swap_dot.wait_send()
    for d in range(2):
        for hop in range(half):
            kv_sent(d, hop)
        for m in range(3):
            w_own(d, m).wait_send()
        for k in range(nk - 3):
            sent(w_leaves(d, k), wgt_s.at[d, k + 3])
        for k in range(nk):
            sent(w_arrives(d, k, c), wsb_s.at[d, k])
        for t in range(half):
            grad_copy(d, t).wait_send()
    for m in range(3):
        w_own_sibling(m).wait_send()
    loop(1, ne, lambda p: token_copy(p).wait_send())
    for i in range(parts):
        loop(1, ne, lambda p: ret_copy(i, p).wait_send())
    dq_mine.wait()
    dq_theirs.wait_send()
    arrived(dq_out.at[0, :, their_heads], sib_r.at[5])
    for i, out in enumerate((dk_out, dv_out)):
        final[2 * i].wait()
        final[2 * i + 1].wait_send()
        arrived(out.at[0, :, their_head], sib_r.at[6 + i])
    for copy in outs:
        copy.wait()


def local(nz, ne, queries, keys, values, attn_out, d_attn, normed, d_moe, ids, route, gate_w, up_w, down_t):
    half = nz // 2
    nk = 3 * half
    heads = queries.shape[2]
    width = heads // 2
    groups = width // HEAD
    model = normed.shape[2]
    rows, hid = gate_w.shape[1:]
    slots = ne * SLOT
    parts = 4
    dma = pltpu.SemaphoreType.DMA
    anywhere = pl.BlockSpec(memory_space=pl.ANY)
    vmem = pl.BlockSpec(memory_space=pltpu.VMEM)
    scratch = [
        pltpu.VMEM((3, 2 * nz, rows, hid), BF16),
        pltpu.VMEM((nz, 2, PAIR, HEAD), BF16),
        pltpu.VMEM((nz, HEAD, PAIR), BF16),
        pltpu.VMEM((PAIR, width), BF16),
        pltpu.VMEM((PAIR, width), BF16),
        pltpu.VMEM((TOK, heads), BF16),
        pltpu.VMEM((TOK, heads), BF16),
        pltpu.VMEM((groups, 8, TOK), F32),
        pltpu.VMEM((groups, 8, PAIR), F32),
        pltpu.VMEM((nz, PAIR, PAIR), F32),
        pltpu.VMEM((nz, 8, PAIR), F32),
        pltpu.VMEM((nz, 2, PAIR, HEAD), F32),
        pltpu.VMEM((HEAD, PAIR), F32),
        pltpu.VMEM((PAIR, width), BF16),
        pltpu.VMEM((2, half, 2, PAIR, HEAD), BF16),
        pltpu.VMEM((2, half, 2, PAIR, HEAD), BF16),
        pltpu.VMEM((2, PAIR, HEAD), BF16),
        pltpu.VMEM((2, TOK, model), BF16),
        pltpu.VMEM((2, slots, model), BF16),
        pltpu.VMEM((2, slots, model), BF16),
        pltpu.VMEM((3, slots, hid), F32),
        pltpu.VMEM((2, slots, hid), BF16),
        pltpu.VMEM((slots, model), BF16),
        pltpu.VMEM((slots, model), BF16),
        pltpu.VMEM((2, TOK, slots), BF16),
        pltpu.VMEM((TOK, model), BF16),
        dma((14 + parts,)),
        dma((8,)), dma((8,)),
        dma((2, nk)), dma((2, nk)),
        dma((2, nk + 3)), dma((2, nk + 3)),
        dma((2, half)), dma((2, half)),
        dma((2, half)), dma((2, half)),
        dma((ne,)), dma((ne,)),
        dma((parts, ne)), dma((parts, ne)),
    ]
    return pl.pallas_call(
        functools.partial(kernel, nz, ne),
        out_shape=(
            jax.ShapeDtypeStruct(queries.shape, BF16),
            jax.ShapeDtypeStruct(keys.shape, BF16),
            jax.ShapeDtypeStruct(values.shape, BF16),
            jax.ShapeDtypeStruct(normed.shape, BF16),
        ),
        in_specs=[anywhere] * 7 + [vmem] * 2 + [anywhere] * 3,
        out_specs=[anywhere] * 4,
        scratch_shapes=scratch,
        compiler_params=pltpu.CompilerParams(
            collective_id=0, has_side_effects=True, vmem_limit_bytes=60 * 1024 * 1024
        ),
        name="layer_backward",
    )(queries, keys, values, attn_out, d_attn, normed, d_moe, ids, route, gate_w, up_w, down_t)


def solution(mesh):
    nz, ne = mesh.shape["seq"] // 2, mesh.shape["exp"]
    spec = P("exp", "seq", None)
    return jax.shard_map(
        functools.partial(local, nz, ne),
        mesh=mesh,
        in_specs=(spec,) * 12,
        out_specs=(spec,) * 4,
        check_vma=False,
    )
```

```python
import functools
import math

import jax
import jax.numpy as jnp
from jax import lax
from jax.experimental import pallas as pl
from jax.experimental.pallas import tpu as pltpu
from jax.sharding import PartitionSpec as P

MESH = pl.DeviceIdType.MESH
F32 = jnp.float32
BF16 = jnp.bfloat16
HEAD = 128
TOK = 128
PAIR = 2 * TOK
SLOT = 16
CAP = 10
LOW = -1e30
PIECES = ((0, 0, 48), (0, 48, 48), (0, 96, 32), (1, 0, 48), (1, 48, 80), (2, 0, 128))
MINOR = (((1,), (1,)), ((), ()))
MAJOR = (((0,), (0,)), ((), ()))


def dot(a, b, dims=(((1,), (0,)), ((), ()))):
    return lax.dot_general(a, b, dims, preferred_element_type=F32)


def kernel(
    nz, ne,
    q_in, k_in, v_in, o_in, do_in, x_in, g_in, ids, route, gate_in, up_in, down_in,
    dq_out, dk_out, dv_out, dn_out,
    W, KV, KT, Q, DO, OF, DOF, RDX, RD, QT, DOT, PB, MJ, ST, DKV, DQT, DQ, SB, RB, FB, XG, XS, XR, ACC, GU, RSF, RSB, RRB, RR, MIX, OUT,
    loc, sib_s, sib_r, own_s, own_r, wgt_s, wgt_r, wsb_s, wsb_r, kv_s, kv_r, gr_s, gr_r, tok_s, tok_r, ret_s, ret_r,
):
    half = nz // 2
    nk = 3 * half
    groups = Q.shape[1] // HEAD
    width = groups * HEAD
    hid = W.shape[3]
    model = W.shape[1] * W.shape[2]
    scale = 1.0 / math.sqrt(HEAD)
    log2e = math.log2(math.e)

    s = lax.axis_index("seq")
    e = lax.axis_index("exp")
    z = lax.div(s, 2)
    c = lax.rem(s, 2)
    other = 1 - c

    def plane(delta):
        return lax.rem(z + delta + nz, nz)

    near = (
        {"seq": 2 * plane(1) + c},
        {"seq": 2 * plane(-1) + c},
    )
    sibling = {"seq": 2 * z + other}

    def peer(p):
        return lax.rem(e + p, ne)

    def send(src, dst, ss, rs, to):
        return pltpu.make_async_remote_copy(
            src_ref=src, dst_ref=dst, send_sem=ss, recv_sem=rs, device_id=to, device_id_type=MESH
        )

    def arrived(dst, rs):
        send(dst, dst, rs, rs, sibling).wait_recv()

    def sent(src, ss):
        send(src, src, ss, ss, sibling).wait_send()

    mine = pl.ds(pl.multiple_of(c * TOK, TOK), TOK)
    theirs = pl.ds(pl.multiple_of(other * TOK, TOK), TOK)
    my_heads = pl.ds(pl.multiple_of(c * width, width), width)
    their_heads = pl.ds(pl.multiple_of(other * width, width), width)
    my_head = pl.ds(pl.multiple_of(c * HEAD, HEAD), HEAD)
    their_head = pl.ds(pl.multiple_of(other * HEAD, HEAD), HEAD)

    local = [
        (k_in.at[0, :, my_head], KV.at[z, 0, mine]),
        (v_in.at[0, :, my_head], KV.at[z, 1, mine]),
        (x_in.at[0], XG.at[0]),
        (g_in.at[0], XG.at[1]),
        (o_in.at[0], OF),
        (do_in.at[0], DOF),
        (q_in.at[0, :, my_heads], Q.at[mine]),
        (do_in.at[0, :, my_heads], DO.at[mine]),
        (gate_in.at[0], W.at[0, s]),
        (up_in.at[0], W.at[1, s]),
        (down_in.at[0], W.at[2, s]),
    ]
    local = [pltpu.make_async_copy(a, b, loc.at[i]) for i, (a, b) in enumerate(local)]
    for copy in local:
        copy.start()

    barrier = pltpu.get_barrier_semaphore()
    for to in (*near, sibling):
        pl.semaphore_signal(barrier, inc=1, device_id=to, device_id_type=MESH)

    def greet(p, carry):
        pl.semaphore_signal(barrier, inc=1, device_id={"exp": peer(p)}, device_id_type=MESH)
        return carry

    lax.fori_loop(1, ne, greet, 0)
    pl.semaphore_wait(barrier, 3 + ne - 1)

    swap = [
        send(k_in.at[0, :, their_head], KV.at[z, 0, mine], sib_s.at[0], sib_r.at[0], sibling),
        send(v_in.at[0, :, their_head], KV.at[z, 1, mine], sib_s.at[1], sib_r.at[1], sibling),
        send(q_in.at[0, :, their_heads], Q.at[mine], sib_s.at[2], sib_r.at[2], sibling),
        send(do_in.at[0, :, their_heads], DO.at[mine], sib_s.at[3], sib_r.at[3], sibling),
    ]
    def kv_region(d, hop):
        at = plane(-hop if d == 0 else hop)
        return KV.at[at] if hop < half else KV.at[at, d]

    def kv_forward(d, hop):
        at = plane(-hop if d == 0 else hop)
        region = KV.at[at] if hop + 1 < half else KV.at[at, d]
        send(region, region, kv_s.at[d, hop], kv_r.at[d, hop], near[d]).start()

    def kv_sent(d, hop):
        at = plane(-hop if d == 0 else hop)
        region = KV.at[at] if hop + 1 < half else KV.at[at, d]
        sent(region, kv_s.at[d, hop])

    def kv_step(hop):
        for d in range(2):
            arrived(kv_region(d, hop), kv_r.at[d, hop - 1])
            if hop < half:
                kv_forward(d, hop)

    own = (gate_in, up_in, down_in)

    def w_own(d, i):
        m, first, rows = PIECES[i]
        part = pl.ds(first, rows)
        return send(own[m].at[0, part], W.at[m, s, part], own_s.at[d, i], own_r.at[d, i], near[d])

    def w_start(i):
        for d in range(2):
            w_own(d, i).start()

    def w_own_sibling(m):
        return send(own[m].at[0], W.at[m, s], wsb_s.at[0, nk + m], wsb_r.at[0, nk + m], sibling)

    def w_region(d, k, core, rows_of=None):
        hop = k // 3 + 1
        at = plane(-hop if d == 0 else hop)
        region = W.at[k % 3, 2 * at + core]
        if rows_of is None:
            return region
        rows = W.shape[2] // 2
        return region.at[pl.ds(rows * rows_of, rows)]

    def w_arrives(d, k, core):
        last = k >= nk - 3
        return w_region(d, k, core, d if last else None)

    def w_leaves(d, k):
        last = k + 3 >= nk - 3
        return w_region(d, k, c, d if last else None)

    def pump(k):
        for d in range(2):
            region = w_arrives(d, k, c)
            if k < 3:
                for i, (m, first, rows) in enumerate(PIECES):
                    if m == k:
                        arrived(region.at[pl.ds(first, rows)], own_r.at[d, i])
            else:
                arrived(region, wgt_r.at[d, k])
            if k + 3 < nk:
                leaving = w_leaves(d, k)
                send(leaving, leaving, wgt_s.at[d, k + 3], wgt_r.at[d, k + 3], near[d]).start()
            send(region, region, wsb_s.at[d, k], wsb_r.at[d, k], sibling).start()

    def routing():
        lane = lax.broadcasted_iota(jnp.int32, (TOK, ne * SLOT), 1)
        expert = lax.shift_right_logical(lane, 4)
        slot = lax.bitwise_and(lane, SLOT - 1).astype(F32)
        named = jnp.zeros((TOK, ne * SLOT), F32)
        weight = jnp.zeros((TOK, ne * SLOT), F32)
        chosen = ids[0].astype(F32).T
        shares = route[0].T
        expert = expert.astype(F32)
        for rank in range(chosen.shape[1]):
            hit = chosen[:, rank : rank + 1] == expert
            named = jnp.where(hit, 1.0, named)
            weight = jnp.where(hit, shares[:, rank : rank + 1], weight)
        row = lax.broadcasted_iota(jnp.int32, (TOK, TOK), 0)
        col = lax.broadcasted_iota(jnp.int32, (TOK, TOK), 1)
        earlier = (col < row).astype(F32).astype(BF16)
        place = dot(earlier, named.astype(BF16))
        select = jnp.where((named > 0.0) & (place == slot), 1.0, 0.0)
        mixing = select * weight
        high = mixing.astype(BF16)
        MIX[0] = high
        MIX[1] = (mixing - high.astype(F32)).astype(BF16)
        return select.astype(BF16)

    def token_copy(p):
        to = peer(p)
        return send(
            XS.at[:, pl.ds(pl.multiple_of(to * SLOT, SLOT), SLOT)],
            XR.at[:, pl.ds(pl.multiple_of(e * SLOT, SLOT), SLOT)],
            tok_s.at[p], tok_r.at[p], {"exp": to},
        )

    def token_arrived(p):
        src = lax.rem(e - p + ne, ne)
        arrived(XR.at[:, pl.ds(pl.multiple_of(src * SLOT, SLOT), SLOT)], tok_r.at[p])

    def loop(lo, hi, f):
        def body(i, carry):
            f(i)
            return carry

        lax.fori_loop(lo, hi, body, 0)

    swap[0].start()
    swap[1].start()
    w_start(0)
    swap[2].start()
    swap[3].start()
    local[0].wait()
    local[1].wait()
    arrived(KV.at[z, 0, theirs], sib_r.at[0])
    arrived(KV.at[z, 1, theirs], sib_r.at[1])
    for d in range(2):
        kv_forward(d, 0)
    w_start(1)
    for m in range(3):
        w_own_sibling(m).start()

    local[4].wait()
    local[5].wait()
    ones = jnp.ones((8, HEAD), BF16)

    def head_dot(col):
        cols = pl.ds(pl.multiple_of(col, HEAD), HEAD)
        product = OF[:, cols].astype(F32) * DOF[:, cols].astype(F32)
        high = product.astype(BF16)
        low = (product - high.astype(F32)).astype(BF16)
        return dot(ones, high, MINOR) + dot(ones, low, MINOR)

    def their_dots(h):
        RDX[h] = head_dot((other * groups + h) * HEAD)

    def my_dots(h):
        RD[h, :, mine] = head_dot((c * groups + h) * HEAD)

    loop(0, groups, their_dots)
    swap_dot = send(RDX, RD.at[:, :, mine], sib_s.at[4], sib_r.at[4], sibling)
    swap_dot.start()
    kv_step(1)
    w_start(2)
    loop(0, groups, my_dots)
    kv_step(2)
    w_start(3)
    local[2].wait()
    local[3].wait()
    select = routing()
    for i in range(2):
        for n in range(model // 512):
            cols = pl.ds(512 * n, 512)
            XS[i, :, cols] = dot(select, XG[i, :, cols], MAJOR).astype(BF16)
    my_slots = pl.ds(pl.multiple_of(e * SLOT, SLOT), SLOT)
    XR[:, my_slots, :] = XS[:, my_slots, :]
    for hop in range(3, half):
        kv_step(hop)
    w_start(4)
    w_start(5)
    DKV[...] = jnp.zeros(DKV.shape, F32)

    def turn(j):
        KT[j] = KV[j, 0].T

    pump(0)
    if half > 2:
        kv_step(half)
    loop(0, nz, turn)
    local[6].wait()
    local[7].wait()
    arrived(Q.at[theirs], sib_r.at[2])
    arrived(DO.at[theirs], sib_r.at[3])
    arrived(RD.at[:, :, theirs], sib_r.at[4])
    pump(1)

    pairs = groups // 2
    last_pair = pairs - 1

    def head_cols(pair, i):
        return pl.ds(pl.multiple_of((2 * pair + i) * HEAD, HEAD), HEAD)

    def flip(pair):
        for i in range(2):
            QT[i] = Q[:, head_cols(pair, i)].T

    def scores(j, carry, into, diagonal):
        out = []
        for i in range(2):
            top, total = carry[i]
            value = dot(KV[j, 0], QT[i]) * (scale * log2e)
            if diagonal:
                key = lax.broadcasted_iota(jnp.int32, (PAIR, PAIR), 0)
                query = lax.broadcasted_iota(jnp.int32, (PAIR, PAIR), 1)
                value = jnp.where(key <= query, value, LOW)
            value = value.reshape(PAIR // 8, 8, PAIR)
            new = jnp.maximum(top, jnp.max(value, axis=0))
            value = jnp.exp2(value - new[None])
            total = total * jnp.exp2(top - new) + jnp.sum(value, axis=0)
            PB[i, j] = value.reshape(PAIR, PAIR)
            MJ[into, i, j] = new
            out.append((new, total))
        return tuple(out)

    def fresh():
        return ((jnp.full((8, PAIR), LOW, F32), jnp.zeros((8, PAIR), F32)),) * 2

    def settle(carry, into):
        for i in range(2):
            top, total = carry[i]
            peak = jnp.max(top, axis=0, keepdims=True)
            total = jnp.sum(total * jnp.exp2(top - peak), axis=0, keepdims=True)
            ST[into, i, 0] = jnp.broadcast_to(peak, (8, PAIR))
            ST[into, i, 1] = jnp.broadcast_to(1.0 / total, (8, PAIR))

    def gradients(j, pair, into):
        weights, lows = [], []
        for i in range(2):
            factor = jnp.exp2(MJ[into, i, j] - ST[into, i, 0]) * ST[into, i, 1]
            weight = PB[i, j].reshape(PAIR // 8, 8, PAIR) * factor[None]
            grad = dot(KV[j, 1], DOT[i]).reshape(PAIR // 8, 8, PAIR)
            low = (weight * (grad - RD[2 * pair + i][None])).reshape(PAIR, PAIR).astype(BF16)
            weights.append(weight.reshape(PAIR, PAIR).astype(BF16))
            lows.append(low)
            DQT[i] += dot(KT[j], low)
        grads = jnp.concatenate([DO[:, head_cols(pair, i)] for i in range(2)], axis=0)
        queries = jnp.concatenate([Q[:, head_cols(pair, i)] for i in range(2)], axis=0)
        DKV[j, 1] += dot(jnp.concatenate(weights, axis=1), grads)
        DKV[j, 0] += dot(jnp.concatenate(lows, axis=1), queries)

    def begin(pair):
        for i in range(2):
            DOT[i] = DO[:, head_cols(pair, i)].T
        DQT[...] = jnp.zeros(DQT.shape, F32)

    def end(pair):
        for i in range(2):
            DQ[:, head_cols(pair, i)] = (DQT[i] * scale).T.astype(BF16)

    def both(pair):
        now = lax.rem(pair, 2)
        flip(pair + 1)
        begin(pair)

        def step(j, carry, diagonal):
            gradients(j, pair, now)
            return scores(j, carry, 1 - now, diagonal)

        carry = lax.fori_loop(0, z, lambda j, x: step(j, x, False), fresh())
        settle(step(z, carry, True), 1 - now)
        end(pair)
        for at, k in schedule.items():

            @pl.when(pair == at)
            def _():
                pump(k)

        for i in (1, 2):

            @pl.when(2 * pair + i < ne)
            def _():
                token_copy(2 * pair + i).start()

    schedule = {0: 2, 2: 3, 3: 4, 4: 5, 5: 6} if nz == 8 else {0: 2}
    in_loop = 2 + len(schedule)
    flip(0)
    carry = lax.fori_loop(0, z, lambda j, x: scores(j, x, 0, False), fresh())
    settle(scores(z, carry, 0, True), 0)
    loop(0, last_pair, both)
    begin(last_pair)
    loop(0, z + 1, lambda j: gradients(j, last_pair, last_pair % 2))
    end(last_pair)
    loop(2 * last_pair + 1, ne, lambda p: token_copy(p).start())

    dq_mine = pltpu.make_async_copy(DQ.at[mine], dq_out.at[0, :, my_heads], loc.at[11])
    dq_theirs = send(DQ.at[theirs], dq_out.at[0, :, my_heads], sib_s.at[5], sib_r.at[5], sibling)
    dq_mine.start()
    dq_theirs.start()

    def grad_step(r):
        for d in range(2):
            t = half - r
            at = plane(r if d == 0 else -r)
            if r == half:
                SB[d, t, d] = DKV[at, d].astype(BF16)
            elif r == half - 1:
                arrived(RB.at[d, t - 1, d], gr_r.at[d, t - 1])
                SB[d, t, d] = (DKV[at, d] + RB[d, t - 1, d].astype(F32)).astype(BF16)
                SB[d, t, 1 - d] = DKV[at, 1 - d].astype(BF16)
            else:
                arrived(RB.at[d, t - 1], gr_r.at[d, t - 1])
                SB[d, t] = (DKV[at] + RB[d, t - 1].astype(F32)).astype(BF16)
            grad_copy(d, t).start()

    def grad_copy(d, t):
        if t == 0:
            return send(SB.at[d, 0, d], RB.at[d, 0, d], gr_s.at[d, 0], gr_r.at[d, 0], near[d])
        return send(SB.at[d, t], RB.at[d, t], gr_s.at[d, t], gr_r.at[d, t], near[d])

    def grad_end():
        t = half - 1
        for d in range(2):
            arrived(RB.at[d, t], gr_r.at[d, t])
        total = DKV[z] + RB[0, t].astype(F32) + RB[1, t].astype(F32)
        FB[0] = (total[0] * scale).astype(BF16)
        FB[1] = total[1].astype(BF16)
        copies = []
        for i, out in enumerate((dk_out, dv_out)):
            copies.append(pltpu.make_async_copy(FB.at[i, mine], out.at[0, :, my_head], loc.at[12 + i]))
            copies.append(send(FB.at[i, theirs], out.at[0, :, my_head], sib_s.at[6 + i], sib_r.at[6 + i], sibling))
        for copy in copies:
            copy.start()
        return copies

    def gather_wait(d, k):
        arrived(w_arrives(d, k, other), wsb_r.at[d, k])

    def add(m, planes, first=False):
        for n in range(hid // 256):
            cols = pl.ds(256 * n, 256)
            total = None if first else ACC[m, :, cols]
            for at in planes:
                part = dot(
                    XR[m // 2, :, pl.ds(pl.multiple_of(at * PAIR, PAIR), PAIR)],
                    W[m, pl.ds(2 * at, 2), :, cols].reshape(PAIR, 256),
                )
                total = part if total is None else total + part
            ACC[m, :, cols] = total

    def add_hop(hop, m):
        k = 3 * (hop - 1) + m
        for d in range(2):
            gather_wait(d, k)
        add(m, [plane(-hop), plane(hop)] if hop < half else [plane(hop)])

    grad_step(half)
    loop(1, ne, token_arrived)
    for m in range(3):
        local[8 + m].wait()
        arrived(W.at[m, 2 * z + other], wsb_r.at[0, nk + m])
        add(m, [z], first=True)
    hops = [(hop, m) for hop in range(1, half + 1) for m in range(3)]
    done = 0
    for k in range(in_loop, nk):
        pump(k)
        if k == max(nk - 4, in_loop):
            grad_step(half - 1)
        if k == nk - 2 and half > 2:
            grad_step(half - 2)
        while done < k and (done < nk - 4 or k >= nk - 3):
            add_hop(*hops[done])
            done += 1
            if done % 3 == 0 and k < nk - 3:
                break
    while done < nk:
        add_hop(*hops[done])
        done += 1
    if half > 3:
        grad_step(half - 3)

    rows = 16

    def activate(i):
        at = pl.ds(pl.multiple_of(i * rows, rows), rows)
        gate, up, grad = ACC[0, at, :], ACC[1, at, :], ACC[2, at, :]
        sig = 1.0 / (1.0 + jnp.exp(-gate))
        GU[0, at, :] = (grad * up * sig * (1.0 + gate * (1.0 - sig))).astype(BF16)
        GU[1, at, :] = (grad * (gate * sig)).astype(BF16)

    loop(0, ne * SLOT // rows, activate)

    parts = ret_s.shape[0]
    ready = [min(nz, -(-SLOT * (t + 1) // CAP)) for t in range(parts)]

    def ret_copy(t, p):
        to = peer(p)
        rows = pl.ds(SLOT * t, SLOT)
        return send(RSB.at[to, rows], RRB.at[e, rows], ret_s.at[t, p], ret_r.at[t, p], {"exp": to})

    def ret_arrived(t, p):
        src = lax.rem(e - p + ne, ne)
        arrived(RRB.at[src, pl.ds(SLOT * t, SLOT)], ret_r.at[t, p])

    t = 0
    for n in range(nz):
        back = dot(GU[0], W[0, 2 * n : 2 * n + 2].reshape(PAIR, hid), MINOR) + dot(
            GU[1], W[1, 2 * n : 2 * n + 2].reshape(PAIR, hid), MINOR
        )
        for p in range(ne):
            RSF[p, CAP * n : CAP * n + SLOT, :] = back[SLOT * p : SLOT * p + SLOT]
        while t < parts and ready[t] == n + 1:
            rows = pl.ds(SLOT * t, SLOT)
            RSB[:, rows, :] = RSF[:, rows, :].astype(BF16)
            loop(1, ne, lambda p: ret_copy(t, p).start())
            RRB[e, rows, :] = RSB[e, rows, :]
            t += 1
    final = grad_end()
    outs = []
    row = lax.broadcasted_iota(jnp.int32, (SLOT, PAIR), 0)
    t = 0
    for n in range(nz):
        while t < parts and SLOT * t < CAP * (n + 1):
            loop(1, ne, lambda p: ret_arrived(t, p))
            rows = pl.ds(SLOT * t, SLOT)
            RSF[:, rows, :] = RRB[:, rows, :].astype(F32)
            t += 1
        for p in range(ne):
            slots = RSF[p, CAP * n : CAP * n + SLOT, :]
            RR[SLOT * p : SLOT * p + SLOT, :] = jnp.where(row < CAP, slots, 0.0).astype(BF16)
        back = RR[...]
        cols = pl.ds(PAIR * n, PAIR)
        OUT[:, cols] = (dot(MIX[0], back) + dot(MIX[1], back)).astype(BF16)
        copy = pltpu.make_async_copy(OUT.at[:, cols], dn_out.at[0, :, cols], loc.at[14 + n])
        copy.start()
        outs.append(copy)

    for copy in swap:
        copy.wait_send()
    swap_dot.wait_send()
    for d in range(2):
        for hop in range(half):
            kv_sent(d, hop)
        for i in range(len(PIECES)):
            w_own(d, i).wait_send()
        for k in range(nk - 3):
            sent(w_leaves(d, k), wgt_s.at[d, k + 3])
        for k in range(nk):
            sent(w_arrives(d, k, c), wsb_s.at[d, k])
        for t in range(half):
            grad_copy(d, t).wait_send()
    for m in range(3):
        w_own_sibling(m).wait_send()
    loop(1, ne, lambda p: token_copy(p).wait_send())
    for t in range(parts):
        loop(1, ne, lambda p: ret_copy(t, p).wait_send())
    dq_mine.wait()
    dq_theirs.wait_send()
    arrived(dq_out.at[0, :, their_heads], sib_r.at[5])
    for i, out in enumerate((dk_out, dv_out)):
        final[2 * i].wait()
        final[2 * i + 1].wait_send()
        arrived(out.at[0, :, their_head], sib_r.at[6 + i])
    for copy in outs:
        copy.wait()


def local(nz, ne, queries, keys, values, attn_out, d_attn, normed, d_moe, ids, route, gate_w, up_w, down_t):
    half = nz // 2
    nk = 3 * half
    heads = queries.shape[2]
    width = heads // 2
    groups = width // HEAD
    model = normed.shape[2]
    rows, hid = gate_w.shape[1:]
    slots = ne * SLOT
    parts = -(-CAP * nz // SLOT)
    dma = pltpu.SemaphoreType.DMA
    anywhere = pl.BlockSpec(memory_space=pl.ANY)
    vmem = pl.BlockSpec(memory_space=pltpu.VMEM)
    scratch = [
        pltpu.VMEM((3, 2 * nz, rows, hid), BF16),
        pltpu.VMEM((nz, 2, PAIR, HEAD), BF16),
        pltpu.VMEM((nz, HEAD, PAIR), BF16),
        pltpu.VMEM((PAIR, width), BF16),
        pltpu.VMEM((PAIR, width), BF16),
        pltpu.VMEM((TOK, heads), BF16),
        pltpu.VMEM((TOK, heads), BF16),
        pltpu.VMEM((groups, 8, TOK), F32),
        pltpu.VMEM((groups, 8, PAIR), F32),
        pltpu.VMEM((2, HEAD, PAIR), BF16),
        pltpu.VMEM((2, HEAD, PAIR), BF16),
        pltpu.VMEM((2, nz, PAIR, PAIR), F32),
        pltpu.VMEM((2, 2, nz, 8, PAIR), F32),
        pltpu.VMEM((2, 2, 2, 8, PAIR), F32),
        pltpu.VMEM((nz, 2, PAIR, HEAD), F32),
        pltpu.VMEM((2, HEAD, PAIR), F32),
        pltpu.VMEM((PAIR, width), BF16),
        pltpu.VMEM((2, half, 2, PAIR, HEAD), BF16),
        pltpu.VMEM((2, half, 2, PAIR, HEAD), BF16),
        pltpu.VMEM((2, PAIR, HEAD), BF16),
        pltpu.VMEM((2, TOK, model), BF16),
        pltpu.VMEM((2, slots, model), BF16),
        pltpu.VMEM((2, slots, model), BF16),
        pltpu.VMEM((3, slots, hid), F32),
        pltpu.VMEM((2, slots, hid), BF16),
        pltpu.VMEM((ne, SLOT * parts + 8, PAIR), F32),
        pltpu.VMEM((ne, SLOT * parts, PAIR), BF16),
        pltpu.VMEM((ne, SLOT * parts, PAIR), BF16),
        pltpu.VMEM((slots, PAIR), BF16),
        pltpu.VMEM((2, TOK, slots), BF16),
        pltpu.VMEM((TOK, model), BF16),
        dma((14 + nz,)),
        dma((8,)), dma((8,)),
        dma((2, len(PIECES))), dma((2, len(PIECES))),
        dma((2, nk)), dma((2, nk)),
        dma((2, nk + 3)), dma((2, nk + 3)),
        dma((2, half)), dma((2, half)),
        dma((2, half)), dma((2, half)),
        dma((ne,)), dma((ne,)),
        dma((parts, ne)), dma((parts, ne)),
    ]
    return pl.pallas_call(
        functools.partial(kernel, nz, ne),
        out_shape=(
            jax.ShapeDtypeStruct(queries.shape, BF16),
            jax.ShapeDtypeStruct(keys.shape, BF16),
            jax.ShapeDtypeStruct(values.shape, BF16),
            jax.ShapeDtypeStruct(normed.shape, BF16),
        ),
        in_specs=[anywhere] * 7 + [vmem] * 2 + [anywhere] * 3,
        out_specs=[anywhere] * 4,
        scratch_shapes=scratch,
        compiler_params=pltpu.CompilerParams(
            collective_id=0, has_side_effects=True, vmem_limit_bytes=62 * 1024 * 1024
        ),
        name="layer_backward",
    )(queries, keys, values, attn_out, d_attn, normed, d_moe, jnp.swapaxes(ids, 1, 2), jnp.swapaxes(route, 1, 2), gate_w, up_w, down_t)


def solution(mesh):
    nz, ne = mesh.shape["seq"] // 2, mesh.shape["exp"]
    spec = P("exp", "seq", None)
    return jax.shard_map(
        functools.partial(local, nz, ne),
        mesh=mesh,
        in_specs=(spec,) * 12,
        out_specs=(spec,) * 4,
        check_vma=False,
    )
```

```python
import functools
import math

import jax
import jax.numpy as jnp
from jax import lax
from jax.experimental import pallas as pl
from jax.experimental.pallas import tpu as pltpu
from jax.sharding import PartitionSpec as P

MESH = pl.DeviceIdType.MESH
F32 = jnp.float32
BF16 = jnp.bfloat16
HEAD = 128
TOK = 128
PAIR = 2 * TOK
SLOT = 16
CAP = 10
LOW = -1e30
PIECES = ((0, 0, 48), (0, 48, 48), (0, 96, 32), (1, 0, 48), (1, 48, 80), (2, 0, 128))
MINOR = (((1,), (1,)), ((), ()))
MAJOR = (((0,), (0,)), ((), ()))


def dot(a, b, dims=(((1,), (0,)), ((), ()))):
    return lax.dot_general(a, b, dims, preferred_element_type=F32)


def kernel(
    nz, ne,
    q_in, k_in, v_in, o_in, do_in, x_in, g_in, ids, route, gate_in, up_in, down_in,
    dq_out, dk_out, dv_out, dn_out,
    W, KV, KT, Q, DO, OF, DOF, RDX, RD, QT, DOT, PB, MJ, ST, DKV, DQT, DQ, SB, RB, FB, XG, XS, XR, ACC, GU, RSF, RSB, RRB, RR, MIX, OUT,
    loc, sib_s, sib_r, own_s, own_r, wgt_s, wgt_r, wsb_s, wsb_r, kv_s, kv_r, gr_s, gr_r, tok_s, tok_r, ret_s, ret_r,
):
    half = nz // 2
    nk = 3 * half
    groups = Q.shape[1] // HEAD
    width = groups * HEAD
    hid = W.shape[3]
    model = W.shape[1] * W.shape[2]
    scale = 1.0 / math.sqrt(HEAD)
    log2e = math.log2(math.e)

    s = lax.axis_index("seq")
    e = lax.axis_index("exp")
    z = lax.div(s, 2)
    c = lax.rem(s, 2)
    other = 1 - c

    def plane(delta):
        return lax.rem(z + delta + nz, nz)

    near = (
        {"seq": 2 * plane(1) + c},
        {"seq": 2 * plane(-1) + c},
    )
    sibling = {"seq": 2 * z + other}

    def peer(p):
        return lax.rem(e + p, ne)

    def send(src, dst, ss, rs, to):
        return pltpu.make_async_remote_copy(
            src_ref=src, dst_ref=dst, send_sem=ss, recv_sem=rs, device_id=to, device_id_type=MESH
        )

    def arrived(dst, rs):
        send(dst, dst, rs, rs, sibling).wait_recv()

    def sent(src, ss):
        send(src, src, ss, ss, sibling).wait_send()

    mine = pl.ds(pl.multiple_of(c * TOK, TOK), TOK)
    theirs = pl.ds(pl.multiple_of(other * TOK, TOK), TOK)
    my_heads = pl.ds(pl.multiple_of(c * width, width), width)
    their_heads = pl.ds(pl.multiple_of(other * width, width), width)
    my_head = pl.ds(pl.multiple_of(c * HEAD, HEAD), HEAD)
    their_head = pl.ds(pl.multiple_of(other * HEAD, HEAD), HEAD)

    local = [
        (k_in.at[0, :, my_head], KV.at[z, 0, mine]),
        (v_in.at[0, :, my_head], KV.at[z, 1, mine]),
        (x_in.at[0], XG.at[0]),
        (g_in.at[0], XG.at[1]),
        (o_in.at[0], OF),
        (do_in.at[0], DOF),
        (q_in.at[0, :, my_heads], Q.at[mine]),
        (do_in.at[0, :, my_heads], DO.at[mine]),
        (gate_in.at[0], W.at[0, s]),
        (up_in.at[0], W.at[1, s]),
        (down_in.at[0], W.at[2, s]),
    ]
    local = [pltpu.make_async_copy(a, b, loc.at[i]) for i, (a, b) in enumerate(local)]
    for copy in local[:2]:
        copy.start()

    barrier = pltpu.get_barrier_semaphore()
    for to in (*near, sibling):
        pl.semaphore_signal(barrier, inc=1, device_id=to, device_id_type=MESH)

    def greet(p, carry):
        pl.semaphore_signal(barrier, inc=1, device_id={"exp": peer(p)}, device_id_type=MESH)
        return carry

    lax.fori_loop(1, ne, greet, 0)
    pl.semaphore_wait(barrier, 3 + ne - 1)

    swap = [
        send(k_in.at[0, :, their_head], KV.at[z, 0, mine], sib_s.at[0], sib_r.at[0], sibling),
        send(v_in.at[0, :, their_head], KV.at[z, 1, mine], sib_s.at[1], sib_r.at[1], sibling),
        send(q_in.at[0, :, their_heads], Q.at[mine], sib_s.at[2], sib_r.at[2], sibling),
        send(do_in.at[0, :, their_heads], DO.at[mine], sib_s.at[3], sib_r.at[3], sibling),
    ]
    def kv_region(d, hop):
        at = plane(-hop if d == 0 else hop)
        return KV.at[at] if hop < half else KV.at[at, d]

    def kv_forward(d, hop):
        at = plane(-hop if d == 0 else hop)
        region = KV.at[at] if hop + 1 < half else KV.at[at, d]
        send(region, region, kv_s.at[d, hop], kv_r.at[d, hop], near[d]).start()

    def kv_sent(d, hop):
        at = plane(-hop if d == 0 else hop)
        region = KV.at[at] if hop + 1 < half else KV.at[at, d]
        sent(region, kv_s.at[d, hop])

    def kv_step(hop):
        for d in range(2):
            arrived(kv_region(d, hop), kv_r.at[d, hop - 1])
            if hop < half:
                kv_forward(d, hop)

    own = (gate_in, up_in, down_in)

    def w_own(d, i):
        m, first, rows = PIECES[i]
        part = pl.ds(first, rows)
        return send(own[m].at[0, part], W.at[m, s, part], own_s.at[d, i], own_r.at[d, i], near[d])

    def w_start(i):
        for d in range(2):
            w_own(d, i).start()

    def w_own_sibling(m):
        return send(own[m].at[0], W.at[m, s], wsb_s.at[0, nk + m], wsb_r.at[0, nk + m], sibling)

    def w_region(d, k, core, rows_of=None):
        hop = k // 3 + 1
        at = plane(-hop if d == 0 else hop)
        region = W.at[k % 3, 2 * at + core]
        if rows_of is None:
            return region
        rows = W.shape[2] // 2
        return region.at[pl.ds(rows * rows_of, rows)]

    def w_arrives(d, k, core):
        last = k >= nk - 3
        return w_region(d, k, core, d if last else None)

    def w_leaves(d, k):
        last = k + 3 >= nk - 3
        return w_region(d, k, c, d if last else None)

    def pump(k):
        for d in range(2):
            region = w_arrives(d, k, c)
            if k < 3:
                for i, (m, first, rows) in enumerate(PIECES):
                    if m == k:
                        arrived(region.at[pl.ds(first, rows)], own_r.at[d, i])
            else:
                arrived(region, wgt_r.at[d, k])
            if k + 3 < nk:
                leaving = w_leaves(d, k)
                send(leaving, leaving, wgt_s.at[d, k + 3], wgt_r.at[d, k + 3], near[d]).start()
            send(region, region, wsb_s.at[d, k], wsb_r.at[d, k], sibling).start()

    def routing():
        lane = lax.broadcasted_iota(jnp.int32, (TOK, ne * SLOT), 1)
        expert = lax.shift_right_logical(lane, 4)
        slot = lax.bitwise_and(lane, SLOT - 1).astype(F32)
        named = jnp.zeros((TOK, ne * SLOT), F32)
        weight = jnp.zeros((TOK, ne * SLOT), F32)
        chosen = ids[0].astype(F32).T
        shares = route[0].T
        expert = expert.astype(F32)
        for rank in range(chosen.shape[1]):
            hit = chosen[:, rank : rank + 1] == expert
            named = jnp.where(hit, 1.0, named)
            weight = jnp.where(hit, shares[:, rank : rank + 1], weight)
        row = lax.broadcasted_iota(jnp.int32, (TOK, TOK), 0)
        col = lax.broadcasted_iota(jnp.int32, (TOK, TOK), 1)
        earlier = (col < row).astype(F32).astype(BF16)
        place = dot(earlier, named.astype(BF16))
        select = jnp.where((named > 0.0) & (place == slot), 1.0, 0.0)
        mixing = select * weight
        high = mixing.astype(BF16)
        MIX[0] = high
        MIX[1] = (mixing - high.astype(F32)).astype(BF16)
        return select.astype(BF16)

    def token_copy(p):
        to = peer(p)
        return send(
            XS.at[:, pl.ds(pl.multiple_of(to * SLOT, SLOT), SLOT)],
            XR.at[:, pl.ds(pl.multiple_of(e * SLOT, SLOT), SLOT)],
            tok_s.at[p], tok_r.at[p], {"exp": to},
        )

    def token_arrived(p):
        src = lax.rem(e - p + ne, ne)
        arrived(XR.at[:, pl.ds(pl.multiple_of(src * SLOT, SLOT), SLOT)], tok_r.at[p])

    def loop(lo, hi, f):
        def body(i, carry):
            f(i)
            return carry

        lax.fori_loop(lo, hi, body, 0)

    swap[0].start()
    swap[1].start()
    w_start(0)
    local[0].wait()
    local[1].wait()
    arrived(KV.at[z, 0, theirs], sib_r.at[0])
    arrived(KV.at[z, 1, theirs], sib_r.at[1])
    for d in range(2):
        kv_forward(d, 0)
    w_start(1)
    for copy in local[2:]:
        copy.start()
    swap[2].start()
    swap[3].start()
    for m in range(3):
        w_own_sibling(m).start()

    local[4].wait()
    local[5].wait()
    ones = jnp.ones((8, HEAD), BF16)

    def head_dot(col):
        cols = pl.ds(pl.multiple_of(col, HEAD), HEAD)
        product = OF[:, cols].astype(F32) * DOF[:, cols].astype(F32)
        high = product.astype(BF16)
        low = (product - high.astype(F32)).astype(BF16)
        return dot(ones, high, MINOR) + dot(ones, low, MINOR)

    def their_dots(h):
        RDX[h] = head_dot((other * groups + h) * HEAD)

    def my_dots(h):
        RD[h, :, mine] = head_dot((c * groups + h) * HEAD)

    loop(0, groups, their_dots)
    swap_dot = send(RDX, RD.at[:, :, mine], sib_s.at[4], sib_r.at[4], sibling)
    swap_dot.start()
    kv_step(1)
    w_start(2)
    loop(0, groups, my_dots)
    kv_step(2)
    w_start(3)
    local[2].wait()
    local[3].wait()
    select = routing()
    for i in range(2):
        for n in range(model // 512):
            cols = pl.ds(512 * n, 512)
            XS[i, :, cols] = dot(select, XG[i, :, cols], MAJOR).astype(BF16)
    my_slots = pl.ds(pl.multiple_of(e * SLOT, SLOT), SLOT)
    XR[:, my_slots, :] = XS[:, my_slots, :]
    for hop in range(3, half):
        kv_step(hop)
    w_start(4)
    w_start(5)
    DKV[...] = jnp.zeros(DKV.shape, F32)

    def turn(j):
        KT[j] = KV[j, 0].T

    pump(0)
    if half > 2:
        kv_step(half)
    loop(0, nz, turn)
    local[6].wait()
    local[7].wait()
    arrived(Q.at[theirs], sib_r.at[2])
    arrived(DO.at[theirs], sib_r.at[3])
    arrived(RD.at[:, :, theirs], sib_r.at[4])
    pump(1)

    pairs = groups // 2
    last_pair = pairs - 1

    def head_cols(pair, i):
        return pl.ds(pl.multiple_of((2 * pair + i) * HEAD, HEAD), HEAD)

    def flip(pair):
        for i in range(2):
            QT[i] = Q[:, head_cols(pair, i)].T

    def scores(j, carry, into, diagonal):
        out = []
        for i in range(2):
            top, total = carry[i]
            value = dot(KV[j, 0], QT[i]) * (scale * log2e)
            if diagonal:
                key = lax.broadcasted_iota(jnp.int32, (PAIR, PAIR), 0)
                query = lax.broadcasted_iota(jnp.int32, (PAIR, PAIR), 1)
                value = jnp.where(key <= query, value, LOW)
            value = value.reshape(PAIR // 8, 8, PAIR)
            new = jnp.maximum(top, jnp.max(value, axis=0))
            value = jnp.exp2(value - new[None])
            total = total * jnp.exp2(top - new) + jnp.sum(value, axis=0)
            PB[i, j] = value.reshape(PAIR, PAIR)
            MJ[into, i, j] = new
            out.append((new, total))
        return tuple(out)

    def fresh():
        return ((jnp.full((8, PAIR), LOW, F32), jnp.zeros((8, PAIR), F32)),) * 2

    def settle(carry, into):
        for i in range(2):
            top, total = carry[i]
            peak = jnp.max(top, axis=0, keepdims=True)
            total = jnp.sum(total * jnp.exp2(top - peak), axis=0, keepdims=True)
            ST[into, i, 0] = jnp.broadcast_to(peak, (8, PAIR))
            ST[into, i, 1] = jnp.broadcast_to(1.0 / total, (8, PAIR))

    def gradients(j, pair, into):
        weights, lows = [], []
        for i in range(2):
            factor = jnp.exp2(MJ[into, i, j] - ST[into, i, 0]) * ST[into, i, 1]
            weight = PB[i, j].reshape(PAIR // 8, 8, PAIR) * factor[None]
            grad = dot(KV[j, 1], DOT[i]).reshape(PAIR // 8, 8, PAIR)
            low = (weight * (grad - RD[2 * pair + i][None])).reshape(PAIR, PAIR).astype(BF16)
            weights.append(weight.reshape(PAIR, PAIR).astype(BF16))
            lows.append(low)
            DQT[i] += dot(KT[j], low)
        grads = jnp.concatenate([DO[:, head_cols(pair, i)] for i in range(2)], axis=0)
        queries = jnp.concatenate([Q[:, head_cols(pair, i)] for i in range(2)], axis=0)
        DKV[j, 1] += dot(jnp.concatenate(weights, axis=1), grads)
        DKV[j, 0] += dot(jnp.concatenate(lows, axis=1), queries)

    def begin(pair):
        for i in range(2):
            DOT[i] = DO[:, head_cols(pair, i)].T
        DQT[...] = jnp.zeros(DQT.shape, F32)

    def end(pair):
        for i in range(2):
            DQ[:, head_cols(pair, i)] = (DQT[i] * scale).T.astype(BF16)

    def both(pair):
        now = lax.rem(pair, 2)
        flip(pair + 1)
        begin(pair)

        def step(j, carry, diagonal):
            gradients(j, pair, now)
            return scores(j, carry, 1 - now, diagonal)

        carry = lax.fori_loop(0, z, lambda j, x: step(j, x, False), fresh())
        settle(step(z, carry, True), 1 - now)
        end(pair)
        for at, k in schedule.items():

            @pl.when(pair == at)
            def _():
                pump(k)

        for i in (1, 2):

            @pl.when(2 * pair + i < ne)
            def _():
                token_copy(2 * pair + i).start()

    schedule = {0: 2, 2: 3, 3: 4, 4: 5, 5: 6} if nz == 8 else {0: 2}
    in_loop = 2 + len(schedule)
    flip(0)
    carry = lax.fori_loop(0, z, lambda j, x: scores(j, x, 0, False), fresh())
    settle(scores(z, carry, 0, True), 0)
    loop(0, last_pair, both)
    begin(last_pair)
    loop(0, z + 1, lambda j: gradients(j, last_pair, last_pair % 2))
    end(last_pair)
    loop(2 * last_pair + 1, ne, lambda p: token_copy(p).start())

    dq_mine = pltpu.make_async_copy(DQ.at[mine], dq_out.at[0, :, my_heads], loc.at[11])
    dq_theirs = send(DQ.at[theirs], dq_out.at[0, :, my_heads], sib_s.at[5], sib_r.at[5], sibling)
    dq_mine.start()
    dq_theirs.start()

    def grad_step(r):
        for d in range(2):
            t = half - r
            at = plane(r if d == 0 else -r)
            if r == half:
                SB[d, t, d] = DKV[at, d].astype(BF16)
            elif r == half - 1:
                arrived(RB.at[d, t - 1, d], gr_r.at[d, t - 1])
                SB[d, t, d] = (DKV[at, d] + RB[d, t - 1, d].astype(F32)).astype(BF16)
                SB[d, t, 1 - d] = DKV[at, 1 - d].astype(BF16)
            else:
                arrived(RB.at[d, t - 1], gr_r.at[d, t - 1])
                SB[d, t] = (DKV[at] + RB[d, t - 1].astype(F32)).astype(BF16)
            grad_copy(d, t).start()

    def grad_copy(d, t):
        if t == 0:
            return send(SB.at[d, 0, d], RB.at[d, 0, d], gr_s.at[d, 0], gr_r.at[d, 0], near[d])
        return send(SB.at[d, t], RB.at[d, t], gr_s.at[d, t], gr_r.at[d, t], near[d])

    def grad_end():
        t = half - 1
        for d in range(2):
            arrived(RB.at[d, t], gr_r.at[d, t])
        total = DKV[z] + RB[0, t].astype(F32) + RB[1, t].astype(F32)
        FB[0] = (total[0] * scale).astype(BF16)
        FB[1] = total[1].astype(BF16)
        copies = []
        for i, out in enumerate((dk_out, dv_out)):
            copies.append(pltpu.make_async_copy(FB.at[i, mine], out.at[0, :, my_head], loc.at[12 + i]))
            copies.append(send(FB.at[i, theirs], out.at[0, :, my_head], sib_s.at[6 + i], sib_r.at[6 + i], sibling))
        for copy in copies:
            copy.start()
        return copies

    def gather_wait(d, k):
        arrived(w_arrives(d, k, other), wsb_r.at[d, k])

    def add(m, planes, first=False):
        for n in range(hid // 256):
            cols = pl.ds(256 * n, 256)
            total = None if first else ACC[m, :, cols]
            for at in planes:
                part = dot(
                    XR[m // 2, :, pl.ds(pl.multiple_of(at * PAIR, PAIR), PAIR)],
                    W[m, pl.ds(2 * at, 2), :, cols].reshape(PAIR, 256),
                )
                total = part if total is None else total + part
            ACC[m, :, cols] = total

    def add_hop(hop, m):
        k = 3 * (hop - 1) + m
        for d in range(2):
            gather_wait(d, k)
        add(m, [plane(-hop), plane(hop)] if hop < half else [plane(hop)])

    grad_step(half)
    loop(1, ne, token_arrived)
    for m in range(3):
        local[8 + m].wait()
        arrived(W.at[m, 2 * z + other], wsb_r.at[0, nk + m])
        add(m, [z], first=True)
    hops = [(hop, m) for hop in range(1, half + 1) for m in range(3)]
    done = 0
    rows = 16

    def prepare(i):
        at = pl.ds(pl.multiple_of(i * rows, rows), rows)
        gate, up = ACC[0, at, :], ACC[1, at, :]
        sig = 1.0 / (1.0 + jnp.exp(-gate))
        ACC[0, at, :] = up * sig * (1.0 + gate * (1.0 - sig))
        ACC[1, at, :] = gate * sig

    for k in range(in_loop, nk):
        if k == nk - 1:
            while done < k:
                add_hop(*hops[done])
                done += 1
            loop(0, ne * SLOT // rows, prepare)
        pump(k)
        if k == nk - 1:
            grad_step(half - 1)
        while done < k and (done < nk - 4 or k >= nk - 3):
            add_hop(*hops[done])
            done += 1
            if done % 3 == 0 and k < nk - 3:
                break
    while done < nk:
        add_hop(*hops[done])
        done += 1
    if half > 2:
        grad_step(half - 2)

    def activate(i):
        at = pl.ds(pl.multiple_of(i * rows, rows), rows)
        grad = ACC[2, at, :]
        GU[0, at, :] = (grad * ACC[0, at, :]).astype(BF16)
        GU[1, at, :] = (grad * ACC[1, at, :]).astype(BF16)

    loop(0, ne * SLOT // rows, activate)

    parts = ret_s.shape[0]
    tiles = RSB.shape[1] // SLOT
    first = [2 * t for t in range(parts)] + [tiles]
    ready = [min(nz, -(-SLOT * first[t + 1] // CAP)) for t in range(parts)]

    def ret_rows(t):
        return pl.ds(SLOT * first[t], SLOT * (first[t + 1] - first[t]))

    def ret_copy(t, p):
        to = peer(p)
        rows = ret_rows(t)
        return send(RSB.at[to, rows], RRB.at[e, rows], ret_s.at[t, p], ret_r.at[t, p], {"exp": to})

    def ret_arrived(t, p):
        src = lax.rem(e - p + ne, ne)
        arrived(RRB.at[src, ret_rows(t)], ret_r.at[t, p])

    t = 0
    for n in range(nz):
        back = dot(GU[0], W[0, 2 * n : 2 * n + 2].reshape(PAIR, hid), MINOR) + dot(
            GU[1], W[1, 2 * n : 2 * n + 2].reshape(PAIR, hid), MINOR
        )
        for p in range(ne):
            RSF[p, CAP * n : CAP * n + SLOT, :] = back[SLOT * p : SLOT * p + SLOT]
        if n == 4 and half > 3:
            grad_step(half - 3)
        while t < parts and ready[t] == n + 1:
            rows = ret_rows(t)
            RSB[:, rows, :] = RSF[:, rows, :].astype(BF16)
            loop(1, ne, lambda p: ret_copy(t, p).start())
            RRB[e, rows, :] = RSB[e, rows, :]
            t += 1
    final = grad_end()
    outs = []
    row = lax.broadcasted_iota(jnp.int32, (SLOT, PAIR), 0)
    t = 0
    for n in range(nz):
        while t < parts and SLOT * first[t] < CAP * (n + 1):
            loop(1, ne, lambda p: ret_arrived(t, p))
            rows = ret_rows(t)
            RSF[:, rows, :] = RRB[:, rows, :].astype(F32)
            t += 1
        for p in range(ne):
            slots = RSF[p, CAP * n : CAP * n + SLOT, :]
            RR[SLOT * p : SLOT * p + SLOT, :] = jnp.where(row < CAP, slots, 0.0).astype(BF16)
        back = RR[...]
        cols = pl.ds(PAIR * n, PAIR)
        OUT[:, cols] = (dot(MIX[0], back) + dot(MIX[1], back)).astype(BF16)
        copy = pltpu.make_async_copy(OUT.at[:, cols], dn_out.at[0, :, cols], loc.at[14 + n])
        copy.start()
        outs.append(copy)

    for copy in swap:
        copy.wait_send()
    swap_dot.wait_send()
    for d in range(2):
        for hop in range(half):
            kv_sent(d, hop)
        for i in range(len(PIECES)):
            w_own(d, i).wait_send()
        for k in range(nk - 3):
            sent(w_leaves(d, k), wgt_s.at[d, k + 3])
        for k in range(nk):
            sent(w_arrives(d, k, c), wsb_s.at[d, k])
        for t in range(half):
            grad_copy(d, t).wait_send()
    for m in range(3):
        w_own_sibling(m).wait_send()
    loop(1, ne, lambda p: token_copy(p).wait_send())
    for t in range(parts):
        loop(1, ne, lambda p: ret_copy(t, p).wait_send())
    dq_mine.wait()
    dq_theirs.wait_send()
    arrived(dq_out.at[0, :, their_heads], sib_r.at[5])
    for i, out in enumerate((dk_out, dv_out)):
        final[2 * i].wait()
        final[2 * i + 1].wait_send()
        arrived(out.at[0, :, their_head], sib_r.at[6 + i])
    for copy in outs:
        copy.wait()


def hand_over(*refs):
    for src, dst in zip(refs[:4], refs[4:]):
        dst[...] = src[...]


def local(nz, ne, queries, keys, values, attn_out, d_attn, normed, d_moe, ids, route, gate_w, up_w, down_t):
    half = nz // 2
    nk = 3 * half
    heads = queries.shape[2]
    width = heads // 2
    groups = width // HEAD
    model = normed.shape[2]
    rows, hid = gate_w.shape[1:]
    slots = ne * SLOT
    tiles = -(-CAP * nz // SLOT)
    parts = -(-tiles // 2)
    dma = pltpu.SemaphoreType.DMA
    anywhere = pl.BlockSpec(memory_space=pl.ANY)
    vmem = pl.BlockSpec(memory_space=pltpu.VMEM)
    scratch = [
        pltpu.VMEM((3, 2 * nz, rows, hid), BF16),
        pltpu.VMEM((nz, 2, PAIR, HEAD), BF16),
        pltpu.VMEM((nz, HEAD, PAIR), BF16),
        pltpu.VMEM((PAIR, width), BF16),
        pltpu.VMEM((PAIR, width), BF16),
        pltpu.VMEM((TOK, heads), BF16),
        pltpu.VMEM((TOK, heads), BF16),
        pltpu.VMEM((groups, 8, TOK), F32),
        pltpu.VMEM((groups, 8, PAIR), F32),
        pltpu.VMEM((2, HEAD, PAIR), BF16),
        pltpu.VMEM((2, HEAD, PAIR), BF16),
        pltpu.VMEM((2, nz, PAIR, PAIR), F32),
        pltpu.VMEM((2, 2, nz, 8, PAIR), F32),
        pltpu.VMEM((2, 2, 2, 8, PAIR), F32),
        pltpu.VMEM((nz, 2, PAIR, HEAD), F32),
        pltpu.VMEM((2, HEAD, PAIR), F32),
        pltpu.VMEM((PAIR, width), BF16),
        pltpu.VMEM((2, half, 2, PAIR, HEAD), BF16),
        pltpu.VMEM((2, half, 2, PAIR, HEAD), BF16),
        pltpu.VMEM((2, PAIR, HEAD), BF16),
        pltpu.VMEM((2, TOK, model), BF16),
        pltpu.VMEM((2, slots, model), BF16),
        pltpu.VMEM((2, slots, model), BF16),
        pltpu.VMEM((3, slots, hid), F32),
        pltpu.VMEM((2, slots, hid), BF16),
        pltpu.VMEM((ne, SLOT * tiles + 8, PAIR), F32),
        pltpu.VMEM((ne, SLOT * tiles, PAIR), BF16),
        pltpu.VMEM((ne, SLOT * tiles, PAIR), BF16),
        pltpu.VMEM((slots, PAIR), BF16),
        pltpu.VMEM((2, TOK, slots), BF16),
        pltpu.VMEM((TOK, model), BF16),
        dma((14 + nz,)),
        dma((8,)), dma((8,)),
        dma((2, len(PIECES))), dma((2, len(PIECES))),
        dma((2, nk)), dma((2, nk)),
        dma((2, nk + 3)), dma((2, nk + 3)),
        dma((2, half)), dma((2, half)),
        dma((2, half)), dma((2, half)),
        dma((ne,)), dma((ne,)),
        dma((parts, ne)), dma((parts, ne)),
    ]
    results = pl.pallas_call(
        functools.partial(kernel, nz, ne),
        out_shape=(
            jax.ShapeDtypeStruct(queries.shape, BF16),
            jax.ShapeDtypeStruct(keys.shape, BF16),
            jax.ShapeDtypeStruct(values.shape, BF16),
            jax.ShapeDtypeStruct(normed.shape, BF16),
        ),
        in_specs=[anywhere] * 7 + [vmem] * 2 + [anywhere] * 3,
        out_specs=[anywhere] * 4,
        scratch_shapes=scratch,
        compiler_params=pltpu.CompilerParams(
            collective_id=0, has_side_effects=True, vmem_limit_bytes=62 * 1024 * 1024
        ),
        name="layer_backward",
    )(queries, keys, values, attn_out, d_attn, normed, d_moe, jnp.swapaxes(ids, 1, 2), jnp.swapaxes(route, 1, 2), gate_w, up_w, down_t)
    return pl.pallas_call(
        hand_over,
        out_shape=tuple(jax.ShapeDtypeStruct(r.shape, BF16) for r in results),
        in_specs=[vmem] * 4,
        out_specs=[vmem] * 4,
        name="hand_over",
    )(*results)


def solution(mesh):
    nz, ne = mesh.shape["seq"] // 2, mesh.shape["exp"]
    spec = P("exp", "seq", None)
    return jax.shard_map(
        functools.partial(local, nz, ne),
        mesh=mesh,
        in_specs=(spec,) * 12,
        out_specs=(spec,) * 4,
        check_vma=False,
    )
```

```python
import functools
import math

import jax
import jax.numpy as jnp
from jax import lax
from jax.experimental import pallas as pl
from jax.experimental.pallas import tpu as pltpu
from jax.sharding import PartitionSpec as P

MESH = pl.DeviceIdType.MESH
F32 = jnp.float32
BF16 = jnp.bfloat16
HEAD = 128
TOK = 128
PAIR = 2 * TOK
SLOT = 16
CAP = 10
LOW = -1e30
PIECES = ((0, 0, 48), (0, 48, 48), (0, 96, 32), (1, 0, 48), (1, 48, 80), (2, 0, 128))
MINOR = (((1,), (1,)), ((), ()))
MAJOR = (((0,), (0,)), ((), ()))


def dot(a, b, dims=(((1,), (0,)), ((), ()))):
    return lax.dot_general(a, b, dims, preferred_element_type=F32)


def kernel(
    nz, ne,
    q_in, k_in, v_in, o_in, do_in, x_in, g_in, ids, route, gate_in, up_in, down_in,
    dq_out, dk_out, dv_out, dn_out,
    W, KV, KT, Q, DO, OF, DOF, RDX, RD, QT, DOT, PB, MJ, ST, DKV, DQT, DQ, SB, RB, FB, XG, XS, XR, ACC, GU, RSF, RSB, RRB, RR, MIX, OUT,
    loc, sib_s, sib_r, own_s, own_r, wgt_s, wgt_r, wsb_s, wsb_r, kv_s, kv_r, gr_s, gr_r, tok_s, tok_r, ret_s, ret_r,
):
    half = nz // 2
    nk = 3 * half
    groups = Q.shape[1] // HEAD
    width = groups * HEAD
    hid = W.shape[3]
    model = W.shape[1] * W.shape[2]
    scale = 1.0 / math.sqrt(HEAD)
    log2e = math.log2(math.e)

    s = lax.axis_index("seq")
    e = lax.axis_index("exp")
    z = lax.div(s, 2)
    c = lax.rem(s, 2)
    other = 1 - c

    def plane(delta):
        return lax.rem(z + delta + nz, nz)

    near = (
        {"seq": 2 * plane(1) + c},
        {"seq": 2 * plane(-1) + c},
    )
    sibling = {"seq": 2 * z + other}

    def peer(p):
        return lax.rem(e + p, ne)

    def send(src, dst, ss, rs, to):
        return pltpu.make_async_remote_copy(
            src_ref=src, dst_ref=dst, send_sem=ss, recv_sem=rs, device_id=to, device_id_type=MESH
        )

    def arrived(dst, rs):
        send(dst, dst, rs, rs, sibling).wait_recv()

    def sent(src, ss):
        send(src, src, ss, ss, sibling).wait_send()

    mine = pl.ds(pl.multiple_of(c * TOK, TOK), TOK)
    theirs = pl.ds(pl.multiple_of(other * TOK, TOK), TOK)
    my_heads = pl.ds(pl.multiple_of(c * width, width), width)
    their_heads = pl.ds(pl.multiple_of(other * width, width), width)
    my_head = pl.ds(pl.multiple_of(c * HEAD, HEAD), HEAD)
    their_head = pl.ds(pl.multiple_of(other * HEAD, HEAD), HEAD)

    local = [
        (k_in.at[0, :, my_head], KV.at[z, 0, mine]),
        (v_in.at[0, :, my_head], KV.at[z, 1, mine]),
        (x_in.at[0], XG.at[0]),
        (g_in.at[0], XG.at[1]),
        (o_in.at[0], OF),
        (do_in.at[0], DOF),
        (q_in.at[0, :, my_heads], Q.at[mine]),
        (do_in.at[0, :, my_heads], DO.at[mine]),
        (gate_in.at[0], W.at[0, s]),
        (up_in.at[0], W.at[1, s]),
        (down_in.at[0], W.at[2, s]),
    ]
    local = [pltpu.make_async_copy(a, b, loc.at[i]) for i, (a, b) in enumerate(local)]
    for copy in local[:2]:
        copy.start()

    barrier = pltpu.get_barrier_semaphore()
    for to in (*near, sibling):
        pl.semaphore_signal(barrier, inc=1, device_id=to, device_id_type=MESH)

    def greet(p, carry):
        pl.semaphore_signal(barrier, inc=1, device_id={"exp": peer(p)}, device_id_type=MESH)
        return carry

    lax.fori_loop(1, ne, greet, 0)
    pl.semaphore_wait(barrier, 3 + ne - 1)

    swap = [
        send(k_in.at[0, :, their_head], KV.at[z, 0, mine], sib_s.at[0], sib_r.at[0], sibling),
        send(v_in.at[0, :, their_head], KV.at[z, 1, mine], sib_s.at[1], sib_r.at[1], sibling),
        send(q_in.at[0, :, their_heads], Q.at[mine], sib_s.at[2], sib_r.at[2], sibling),
        send(do_in.at[0, :, their_heads], DO.at[mine], sib_s.at[3], sib_r.at[3], sibling),
    ]
    def kv_region(d, hop):
        at = plane(-hop if d == 0 else hop)
        return KV.at[at] if hop < half else KV.at[at, d]

    def kv_forward(d, hop):
        at = plane(-hop if d == 0 else hop)
        region = KV.at[at] if hop + 1 < half else KV.at[at, d]
        send(region, region, kv_s.at[d, hop], kv_r.at[d, hop], near[d]).start()

    def kv_sent(d, hop):
        at = plane(-hop if d == 0 else hop)
        region = KV.at[at] if hop + 1 < half else KV.at[at, d]
        sent(region, kv_s.at[d, hop])

    def kv_step(hop):
        for d in range(2):
            arrived(kv_region(d, hop), kv_r.at[d, hop - 1])
            if hop < half:
                kv_forward(d, hop)

    own = (gate_in, up_in, down_in)

    def w_own(d, i):
        m, first, rows = PIECES[i]
        part = pl.ds(first, rows)
        return send(own[m].at[0, part], W.at[m, s, part], own_s.at[d, i], own_r.at[d, i], near[d])

    def w_start(i):
        for d in range(2):
            w_own(d, i).start()

    def w_own_sibling(m):
        return send(own[m].at[0], W.at[m, s], wsb_s.at[0, nk + m], wsb_r.at[0, nk + m], sibling)

    def w_region(d, k, core, rows_of=None):
        hop = k // 3 + 1
        at = plane(-hop if d == 0 else hop)
        region = W.at[k % 3, 2 * at + core]
        if rows_of is None:
            return region
        rows = W.shape[2] // 2
        return region.at[pl.ds(rows * rows_of, rows)]

    def w_arrives(d, k, core):
        last = k >= nk - 3
        return w_region(d, k, core, d if last else None)

    def w_leaves(d, k):
        last = k + 3 >= nk - 3
        return w_region(d, k, c, d if last else None)

    def pump(k):
        for d in range(2):
            region = w_arrives(d, k, c)
            if k < 3:
                for i, (m, first, rows) in enumerate(PIECES):
                    if m == k:
                        arrived(region.at[pl.ds(first, rows)], own_r.at[d, i])
            else:
                arrived(region, wgt_r.at[d, k])
            if k + 3 < nk:
                leaving = w_leaves(d, k)
                send(leaving, leaving, wgt_s.at[d, k + 3], wgt_r.at[d, k + 3], near[d]).start()
            send(region, region, wsb_s.at[d, k], wsb_r.at[d, k], sibling).start()

    def routing():
        lane = lax.broadcasted_iota(jnp.int32, (TOK, ne * SLOT), 1)
        expert = lax.shift_right_logical(lane, 4)
        slot = lax.bitwise_and(lane, SLOT - 1).astype(F32)
        named = jnp.zeros((TOK, ne * SLOT), F32)
        weight = jnp.zeros((TOK, ne * SLOT), F32)
        chosen = ids[0].astype(F32).T
        shares = route[0].T
        expert = expert.astype(F32)
        for rank in range(chosen.shape[1]):
            hit = chosen[:, rank : rank + 1] == expert
            named = jnp.where(hit, 1.0, named)
            weight = jnp.where(hit, shares[:, rank : rank + 1], weight)
        row = lax.broadcasted_iota(jnp.int32, (TOK, TOK), 0)
        col = lax.broadcasted_iota(jnp.int32, (TOK, TOK), 1)
        earlier = (col < row).astype(F32).astype(BF16)
        place = dot(earlier, named.astype(BF16))
        select = jnp.where((named > 0.0) & (place == slot), 1.0, 0.0)
        mixing = select * weight
        high = mixing.astype(BF16)
        MIX[0] = high
        MIX[1] = (mixing - high.astype(F32)).astype(BF16)
        return select.astype(BF16)

    def token_copy(p):
        to = peer(p)
        return send(
            XS.at[:, pl.ds(pl.multiple_of(to * SLOT, SLOT), SLOT)],
            XR.at[:, pl.ds(pl.multiple_of(e * SLOT, SLOT), SLOT)],
            tok_s.at[p], tok_r.at[p], {"exp": to},
        )

    def token_arrived(p):
        src = lax.rem(e - p + ne, ne)
        arrived(XR.at[:, pl.ds(pl.multiple_of(src * SLOT, SLOT), SLOT)], tok_r.at[p])

    def loop(lo, hi, f):
        def body(i, carry):
            f(i)
            return carry

        lax.fori_loop(lo, hi, body, 0)

    swap[0].start()
    swap[1].start()
    w_start(0)
    local[0].wait()
    local[1].wait()
    arrived(KV.at[z, 0, theirs], sib_r.at[0])
    arrived(KV.at[z, 1, theirs], sib_r.at[1])
    for d in range(2):
        kv_forward(d, 0)
    w_start(1)
    for copy in local[2:]:
        copy.start()
    swap[2].start()
    swap[3].start()
    for m in range(3):
        w_own_sibling(m).start()

    local[4].wait()
    local[5].wait()
    ones = jnp.ones((8, HEAD), BF16)

    def head_dot(col):
        cols = pl.ds(pl.multiple_of(col, HEAD), HEAD)
        product = OF[:, cols].astype(F32) * DOF[:, cols].astype(F32)
        high = product.astype(BF16)
        low = (product - high.astype(F32)).astype(BF16)
        return dot(ones, high, MINOR) + dot(ones, low, MINOR)

    def their_dots(h):
        RDX[h] = head_dot((other * groups + h) * HEAD)

    def my_dots(h):
        RD[h, :, mine] = head_dot((c * groups + h) * HEAD)

    loop(0, groups, their_dots)
    swap_dot = send(RDX, RD.at[:, :, mine], sib_s.at[4], sib_r.at[4], sibling)
    swap_dot.start()
    kv_step(1)
    w_start(2)
    loop(0, groups, my_dots)
    kv_step(2)
    w_start(3)
    local[2].wait()
    local[3].wait()
    select = routing()
    for i in range(2):
        for n in range(model // 512):
            cols = pl.ds(512 * n, 512)
            XS[i, :, cols] = dot(select, XG[i, :, cols], MAJOR).astype(BF16)
    my_slots = pl.ds(pl.multiple_of(e * SLOT, SLOT), SLOT)
    XR[:, my_slots, :] = XS[:, my_slots, :]
    for hop in range(3, half):
        kv_step(hop)
    w_start(4)
    w_start(5)
    DKV[...] = jnp.zeros(DKV.shape, F32)

    def turn(j):
        KT[j] = KV[j, 0].T

    pump(0)
    if half > 2:
        kv_step(half)
    loop(0, nz, turn)
    local[6].wait()
    local[7].wait()
    arrived(Q.at[theirs], sib_r.at[2])
    arrived(DO.at[theirs], sib_r.at[3])
    arrived(RD.at[:, :, theirs], sib_r.at[4])
    pump(1)

    pairs = groups // 2
    last_pair = pairs - 1

    def head_cols(pair, i):
        return pl.ds(pl.multiple_of((2 * pair + i) * HEAD, HEAD), HEAD)

    def flip(pair):
        for i in range(2):
            QT[i] = Q[:, head_cols(pair, i)].T

    def scores(j, carry, into, diagonal):
        out = []
        for i in range(2):
            top, total = carry[i]
            value = dot(KV[j, 0], QT[i]) * (scale * log2e)
            if diagonal:
                key = lax.broadcasted_iota(jnp.int32, (PAIR, PAIR), 0)
                query = lax.broadcasted_iota(jnp.int32, (PAIR, PAIR), 1)
                value = jnp.where(key <= query, value, LOW)
            value = value.reshape(PAIR // 8, 8, PAIR)
            new = jnp.maximum(top, jnp.max(value, axis=0))
            value = jnp.exp2(value - new[None])
            total = total * jnp.exp2(top - new) + jnp.sum(value, axis=0)
            PB[i, j] = value.reshape(PAIR, PAIR)
            MJ[into, i, j] = new
            out.append((new, total))
        return tuple(out)

    def fresh():
        return ((jnp.full((8, PAIR), LOW, F32), jnp.zeros((8, PAIR), F32)),) * 2

    def settle(carry, into):
        for i in range(2):
            top, total = carry[i]
            peak = jnp.max(top, axis=0, keepdims=True)
            total = jnp.sum(total * jnp.exp2(top - peak), axis=0, keepdims=True)
            ST[into, i, 0] = jnp.broadcast_to(peak, (8, PAIR))
            ST[into, i, 1] = jnp.broadcast_to(1.0 / total, (8, PAIR))

    def gradients(j, pair, into):
        weights, lows = [], []
        for i in range(2):
            factor = jnp.exp2(MJ[into, i, j] - ST[into, i, 0]) * ST[into, i, 1]
            weight = PB[i, j].reshape(PAIR // 8, 8, PAIR) * factor[None]
            grad = dot(KV[j, 1], DOT[i]).reshape(PAIR // 8, 8, PAIR)
            low = (weight * (grad - RD[2 * pair + i][None])).reshape(PAIR, PAIR).astype(BF16)
            weights.append(weight.reshape(PAIR, PAIR).astype(BF16))
            lows.append(low)
            DQT[i] += dot(KT[j], low)
        grads = jnp.concatenate([DO[:, head_cols(pair, i)] for i in range(2)], axis=0)
        queries = jnp.concatenate([Q[:, head_cols(pair, i)] for i in range(2)], axis=0)
        DKV[j, 1] += dot(jnp.concatenate(weights, axis=1), grads)
        DKV[j, 0] += dot(jnp.concatenate(lows, axis=1), queries)

    def begin(pair):
        for i in range(2):
            DOT[i] = DO[:, head_cols(pair, i)].T
        DQT[...] = jnp.zeros(DQT.shape, F32)

    def end(pair):
        for i in range(2):
            DQ[:, head_cols(pair, i)] = (DQT[i] * scale).T.astype(BF16)

    def both(pair):
        now = lax.rem(pair, 2)
        flip(pair + 1)
        begin(pair)

        def step(j, carry, diagonal):
            gradients(j, pair, now)
            return scores(j, carry, 1 - now, diagonal)

        carry = lax.fori_loop(0, z, lambda j, x: step(j, x, False), fresh())
        settle(step(z, carry, True), 1 - now)
        end(pair)
        for at, k in schedule.items():

            @pl.when(pair == at)
            def _():
                pump(k)

        for i in (1, 2):

            @pl.when(2 * pair + i < ne)
            def _():
                token_copy(2 * pair + i).start()

    schedule = {0: 2, 2: 3, 3: 4, 4: 5, 5: 6} if nz == 8 else {0: 2}
    in_loop = 2 + len(schedule)
    flip(0)
    carry = lax.fori_loop(0, z, lambda j, x: scores(j, x, 0, False), fresh())
    settle(scores(z, carry, 0, True), 0)
    loop(0, last_pair, both)
    pump(in_loop)
    begin(last_pair)
    loop(0, z + 1, lambda j: gradients(j, last_pair, last_pair % 2))
    end(last_pair)
    loop(2 * last_pair + 1, ne, lambda p: token_copy(p).start())

    dq_mine = pltpu.make_async_copy(DQ.at[mine], dq_out.at[0, :, my_heads], loc.at[11])
    dq_theirs = send(DQ.at[theirs], dq_out.at[0, :, my_heads], sib_s.at[5], sib_r.at[5], sibling)
    dq_mine.start()
    dq_theirs.start()

    def grad_step(r):
        for d in range(2):
            t = half - r
            at = plane(r if d == 0 else -r)
            if r == half:
                SB[d, t, d] = DKV[at, d].astype(BF16)
            elif r == half - 1:
                arrived(RB.at[d, t - 1, d], gr_r.at[d, t - 1])
                SB[d, t, d] = (DKV[at, d] + RB[d, t - 1, d].astype(F32)).astype(BF16)
                SB[d, t, 1 - d] = DKV[at, 1 - d].astype(BF16)
            else:
                arrived(RB.at[d, t - 1], gr_r.at[d, t - 1])
                SB[d, t] = (DKV[at] + RB[d, t - 1].astype(F32)).astype(BF16)
            grad_copy(d, t).start()

    def grad_copy(d, t):
        if t == 0:
            return send(SB.at[d, 0, d], RB.at[d, 0, d], gr_s.at[d, 0], gr_r.at[d, 0], near[d])
        return send(SB.at[d, t], RB.at[d, t], gr_s.at[d, t], gr_r.at[d, t], near[d])

    def grad_end():
        t = half - 1
        for d in range(2):
            arrived(RB.at[d, t], gr_r.at[d, t])
        total = DKV[z] + RB[0, t].astype(F32) + RB[1, t].astype(F32)
        FB[0] = (total[0] * scale).astype(BF16)
        FB[1] = total[1].astype(BF16)
        copies = []
        for i, out in enumerate((dk_out, dv_out)):
            copies.append(pltpu.make_async_copy(FB.at[i, mine], out.at[0, :, my_head], loc.at[12 + i]))
            copies.append(send(FB.at[i, theirs], out.at[0, :, my_head], sib_s.at[6 + i], sib_r.at[6 + i], sibling))
        for copy in copies:
            copy.start()
        return copies

    def gather_wait(d, k):
        arrived(w_arrives(d, k, other), wsb_r.at[d, k])

    def add(m, planes, first=False):
        for n in range(hid // 256):
            cols = pl.ds(256 * n, 256)
            total = None if first else ACC[m, :, cols]
            for at in planes:
                part = dot(
                    XR[m // 2, :, pl.ds(pl.multiple_of(at * PAIR, PAIR), PAIR)],
                    W[m, pl.ds(2 * at, 2), :, cols].reshape(PAIR, 256),
                )
                total = part if total is None else total + part
            ACC[m, :, cols] = total

    def add_hop(hop, m):
        k = 3 * (hop - 1) + m
        for d in range(2):
            gather_wait(d, k)
        add(m, [plane(-hop), plane(hop)] if hop < half else [plane(hop)])

    grad_step(half)
    loop(1, ne, token_arrived)
    for m in range(3):
        local[8 + m].wait()
        arrived(W.at[m, 2 * z + other], wsb_r.at[0, nk + m])
        add(m, [z], first=True)
    hops = [(hop, m) for hop in range(1, half + 1) for m in range(3)]
    done = 0
    rows = 16

    def prepare(i):
        at = pl.ds(pl.multiple_of(i * rows, rows), rows)
        gate, up = ACC[0, at, :], ACC[1, at, :]
        sig = 1.0 / (1.0 + jnp.exp(-gate))
        ACC[0, at, :] = up * sig * (1.0 + gate * (1.0 - sig))
        ACC[1, at, :] = gate * sig

    for k in range(in_loop + 1, nk):
        if k == nk - 1:
            while done < k:
                add_hop(*hops[done])
                done += 1
            loop(0, ne * SLOT // rows, prepare)
        pump(k)
        if k == nk - 1:
            grad_step(half - 1)
        while done < k and (done < nk - 4 or k >= nk - 3):
            add_hop(*hops[done])
            done += 1
            if done % 3 == 0 and k < nk - 3:
                break
    while done < nk:
        add_hop(*hops[done])
        done += 1
    if half > 2:
        grad_step(half - 2)

    def activate(i):
        at = pl.ds(pl.multiple_of(i * rows, rows), rows)
        grad = ACC[2, at, :]
        GU[0, at, :] = (grad * ACC[0, at, :]).astype(BF16)
        GU[1, at, :] = (grad * ACC[1, at, :]).astype(BF16)

    loop(0, ne * SLOT // rows, activate)

    parts = ret_s.shape[0]
    tiles = RSB.shape[1] // SLOT
    first = [2 * t for t in range(parts)] + [tiles]
    ready = [min(nz, -(-SLOT * first[t + 1] // CAP)) for t in range(parts)]

    def ret_rows(t):
        return pl.ds(SLOT * first[t], SLOT * (first[t + 1] - first[t]))

    def ret_copy(t, p):
        to = peer(p)
        rows = ret_rows(t)
        return send(RSB.at[to, rows], RRB.at[e, rows], ret_s.at[t, p], ret_r.at[t, p], {"exp": to})

    def ret_arrived(t, p):
        src = lax.rem(e - p + ne, ne)
        arrived(RRB.at[src, ret_rows(t)], ret_r.at[t, p])

    t = 0
    for n in range(nz):
        back = dot(GU[0], W[0, 2 * n : 2 * n + 2].reshape(PAIR, hid), MINOR) + dot(
            GU[1], W[1, 2 * n : 2 * n + 2].reshape(PAIR, hid), MINOR
        )
        for p in range(ne):
            RSF[p, CAP * n : CAP * n + SLOT, :] = back[SLOT * p : SLOT * p + SLOT]
        if n == 4 and half > 3:
            grad_step(half - 3)
        while t < parts and ready[t] == n + 1:
            rows = ret_rows(t)
            RSB[:, rows, :] = RSF[:, rows, :].astype(BF16)
            for p in sorted(range(1, ne), key=lambda p: (p % 4 != 2) + (p // 4 != 2)):
                ret_copy(t, p).start()
            RRB[e, rows, :] = RSB[e, rows, :]
            t += 1
    final = grad_end()
    outs = []
    row = lax.broadcasted_iota(jnp.int32, (SLOT, PAIR), 0)
    t = 0
    for n in range(nz):
        while t < parts and SLOT * first[t] < CAP * (n + 1):
            loop(1, ne, lambda p: ret_arrived(t, p))
            rows = ret_rows(t)
            RSF[:, rows, :] = RRB[:, rows, :].astype(F32)
            t += 1
        for p in range(ne):
            slots = RSF[p, CAP * n : CAP * n + SLOT, :]
            RR[SLOT * p : SLOT * p + SLOT, :] = jnp.where(row < CAP, slots, 0.0).astype(BF16)
        back = RR[...]
        cols = pl.ds(PAIR * n, PAIR)
        OUT[:, cols] = (dot(MIX[0], back) + dot(MIX[1], back)).astype(BF16)
        copy = pltpu.make_async_copy(OUT.at[:, cols], dn_out.at[0, :, cols], loc.at[14 + n])
        copy.start()
        outs.append(copy)

    for copy in swap:
        copy.wait_send()
    swap_dot.wait_send()
    for d in range(2):
        for hop in range(half):
            kv_sent(d, hop)
        for i in range(len(PIECES)):
            w_own(d, i).wait_send()
        for k in range(nk - 3):
            sent(w_leaves(d, k), wgt_s.at[d, k + 3])
        for k in range(nk):
            sent(w_arrives(d, k, c), wsb_s.at[d, k])
        for t in range(half):
            grad_copy(d, t).wait_send()
    for m in range(3):
        w_own_sibling(m).wait_send()
    loop(1, ne, lambda p: token_copy(p).wait_send())
    for t in range(parts):
        loop(1, ne, lambda p: ret_copy(t, p).wait_send())
    dq_mine.wait()
    dq_theirs.wait_send()
    arrived(dq_out.at[0, :, their_heads], sib_r.at[5])
    for i, out in enumerate((dk_out, dv_out)):
        final[2 * i].wait()
        final[2 * i + 1].wait_send()
        arrived(out.at[0, :, their_head], sib_r.at[6 + i])
    for copy in outs:
        copy.wait()


def hand_over(*refs):
    for src, dst in zip(refs[:4], refs[4:]):
        dst[...] = src[...]


def local(nz, ne, queries, keys, values, attn_out, d_attn, normed, d_moe, ids, route, gate_w, up_w, down_t):
    half = nz // 2
    nk = 3 * half
    heads = queries.shape[2]
    width = heads // 2
    groups = width // HEAD
    model = normed.shape[2]
    rows, hid = gate_w.shape[1:]
    slots = ne * SLOT
    tiles = -(-CAP * nz // SLOT)
    parts = -(-tiles // 2)
    dma = pltpu.SemaphoreType.DMA
    anywhere = pl.BlockSpec(memory_space=pl.ANY)
    vmem = pl.BlockSpec(memory_space=pltpu.VMEM)
    scratch = [
        pltpu.VMEM((3, 2 * nz, rows, hid), BF16),
        pltpu.VMEM((nz, 2, PAIR, HEAD), BF16),
        pltpu.VMEM((nz, HEAD, PAIR), BF16),
        pltpu.VMEM((PAIR, width), BF16),
        pltpu.VMEM((PAIR, width), BF16),
        pltpu.VMEM((TOK, heads), BF16),
        pltpu.VMEM((TOK, heads), BF16),
        pltpu.VMEM((groups, 8, TOK), F32),
        pltpu.VMEM((groups, 8, PAIR), F32),
        pltpu.VMEM((2, HEAD, PAIR), BF16),
        pltpu.VMEM((2, HEAD, PAIR), BF16),
        pltpu.VMEM((2, nz, PAIR, PAIR), F32),
        pltpu.VMEM((2, 2, nz, 8, PAIR), F32),
        pltpu.VMEM((2, 2, 2, 8, PAIR), F32),
        pltpu.VMEM((nz, 2, PAIR, HEAD), F32),
        pltpu.VMEM((2, HEAD, PAIR), F32),
        pltpu.VMEM((PAIR, width), BF16),
        pltpu.VMEM((2, half, 2, PAIR, HEAD), BF16),
        pltpu.VMEM((2, half, 2, PAIR, HEAD), BF16),
        pltpu.VMEM((2, PAIR, HEAD), BF16),
        pltpu.VMEM((2, TOK, model), BF16),
        pltpu.VMEM((2, slots, model), BF16),
        pltpu.VMEM((2, slots, model), BF16),
        pltpu.VMEM((3, slots, hid), F32),
        pltpu.VMEM((2, slots, hid), BF16),
        pltpu.VMEM((ne, SLOT * tiles + 8, PAIR), F32),
        pltpu.VMEM((ne, SLOT * tiles, PAIR), BF16),
        pltpu.VMEM((ne, SLOT * tiles, PAIR), BF16),
        pltpu.VMEM((slots, PAIR), BF16),
        pltpu.VMEM((2, TOK, slots), BF16),
        pltpu.VMEM((TOK, model), BF16),
        dma((14 + nz,)),
        dma((8,)), dma((8,)),
        dma((2, len(PIECES))), dma((2, len(PIECES))),
        dma((2, nk)), dma((2, nk)),
        dma((2, nk + 3)), dma((2, nk + 3)),
        dma((2, half)), dma((2, half)),
        dma((2, half)), dma((2, half)),
        dma((ne,)), dma((ne,)),
        dma((parts, ne)), dma((parts, ne)),
    ]
    results = pl.pallas_call(
        functools.partial(kernel, nz, ne),
        out_shape=(
            jax.ShapeDtypeStruct(queries.shape, BF16),
            jax.ShapeDtypeStruct(keys.shape, BF16),
            jax.ShapeDtypeStruct(values.shape, BF16),
            jax.ShapeDtypeStruct(normed.shape, BF16),
        ),
        in_specs=[anywhere] * 7 + [vmem] * 2 + [anywhere] * 3,
        out_specs=[anywhere] * 4,
        scratch_shapes=scratch,
        compiler_params=pltpu.CompilerParams(
            collective_id=0, has_side_effects=True, vmem_limit_bytes=62 * 1024 * 1024
        ),
        name="layer_backward",
    )(queries, keys, values, attn_out, d_attn, normed, d_moe, jnp.swapaxes(ids, 1, 2), jnp.swapaxes(route, 1, 2), gate_w, up_w, down_t)
    return pl.pallas_call(
        hand_over,
        out_shape=tuple(jax.ShapeDtypeStruct(r.shape, BF16) for r in results),
        in_specs=[vmem] * 4,
        out_specs=[vmem] * 4,
        name="hand_over",
    )(*results)


def solution(mesh):
    nz, ne = mesh.shape["seq"] // 2, mesh.shape["exp"]
    spec = P("exp", "seq", None)
    return jax.shard_map(
        functools.partial(local, nz, ne),
        mesh=mesh,
        in_specs=(spec,) * 12,
        out_specs=(spec,) * 4,
        check_vma=False,
    )
```
